32 devices in a mesh: rows: 8 (over z, core), strata: 4 (over y, x).
Axes of the slice: x: 2, y: 2, z: 4, core: 2. Of those that a mesh axis runs over, the one named last changes fastest.
Arguments:
- user_factors: float32 [4096, 512], P(('rows', 'strata')), may hold values from -1.3 to 1.3
- item_factors: float32 [16384, 512], P(('rows', 'strata')), may hold values from -1.3 to 1.3
- ratings: float32 [2, 32768], P(None, ('rows', 'strata')), may hold values from -6 to 6
- user_offsets: int32 [2, 32768], P(None, ('rows', 'strata')), may hold values from 0 to 511, as said below
- item_offsets: int32 [2, 32768], P(None, ('rows', 'strata')), may hold values from 0 to 511
- counts: int32 [2, 32], P(None, ('rows', 'strata')), may hold values from 128 to 1024, as said below
Outputs:
- new_users: float32 [4096, 512], P(('rows', 'strata'))
- new_items: float32 [16384, 512], P(('rows', 'strata'))
The draws below stay inside these ranges and needn't reach their ends.
Inputs may be any that keep to these rules, and one draw needn't show every extreme that they name: `counts`: some tile of each sub-epoch has all 1024 slots active. `user_offsets`: splitting a user block into 4 runs of 128 users, each tile's slots (active or not) name exactly 32 distinct users of every run.
All inputs are finite; a program needn't handle non-finite values.
Results may differ from the reference program's by a relative error of at most 0.0003.
Values sent between devices are 32-bit elements; how exact they have to be, the bound alone decides.
No kernel may reach another device: no remote copies, remote signals or barrier semaphores. Data moves between devices by JAX's collectives and lax.ppermute only.
A program may use at most 64 MiB of HBM per device.

```python
import jax
import jax.numpy as jnp
from jax import lax

K = 512
USER_DEV = 128
TILE_COLS = 512
ENTRIES = 1024
SUBS = 2
TOUCH = 32
USERS = 4096
ITEMS = 16384
N_ROWS = 8
N_STRATA = 4


def draw_counts(key, part):
    first_key = jax.random.fold_in(key, 11)
    second_key = jax.random.fold_in(key, 23)
    device_count = N_ROWS * N_STRATA
    halvings = jax.random.randint(first_key, (SUBS, device_count), 0, 4)
    loads = jnp.right_shift(jnp.full((SUBS, device_count), ENTRIES, jnp.int32), halvings)
    chosen = jax.random.randint(second_key, (SUBS, 1), 0, device_count)
    places = jnp.arange(device_count, dtype=jnp.int32)[None, :]
    return jnp.where(places == chosen, ENTRIES, loads).astype(jnp.int32)


def draw_user_offsets(key, part):
    pick_key = jax.random.fold_in(key, 31)
    order_key = jax.random.fold_in(key, 37)
    fill_key = jax.random.fold_in(key, 41)
    tiles = N_ROWS * N_STRATA
    pairs = N_STRATA * TOUCH
    pick_keys = jax.random.split(pick_key, SUBS * tiles * N_STRATA)
    chosen = jax.vmap(lambda k: jax.random.permutation(k, USER_DEV)[:TOUCH])(pick_keys)
    chosen = chosen.reshape(SUBS, tiles, N_STRATA, TOUCH)
    chosen = chosen + (jnp.arange(N_STRATA, dtype=jnp.int32) * USER_DEV)[None, None, :, None]
    chosen = chosen.reshape(SUBS, tiles, pairs).astype(jnp.int32)
    extra = jax.random.randint(fill_key, (SUBS, tiles, ENTRIES), 0, pairs)
    slots = jnp.arange(ENTRIES, dtype=jnp.int32)[None, None, :]
    base = jnp.where(slots < pairs, slots % pairs, extra).astype(jnp.int32)
    order_keys = jax.random.split(order_key, SUBS * tiles)
    orders = jax.vmap(lambda k: jax.random.permutation(k, ENTRIES))(order_keys).reshape(SUBS, tiles, ENTRIES)
    pair_ids = jnp.take_along_axis(base, orders.astype(jnp.int32), axis=2)
    users = jnp.take_along_axis(chosen, pair_ids, axis=2)
    return users.reshape(SUBS, tiles * ENTRIES).astype(jnp.int32)


def with_ends(values, rng, least, top_value):
    longest = values.shape.index(max(values.shape))
    spots = []
    for shift in (0, 1):
        where = [jax.random.randint(jax.random.fold_in(rng, axis), (), 0, length) for axis, length in enumerate(values.shape)]
        where[longest] = (where[longest] + shift) % values.shape[longest]
        spots.append(tuple(where))
    return values.at[spots[0]].set(least).at[spots[1]].set(top_value)


def block_scale(own_key, dims, shards, least, largest):
    def one(axis_at, shards_of):
        steps = jax.random.uniform(jax.random.fold_in(jax.random.fold_in(own_key, 6), axis_at), (shards_of,), jnp.float32, least / len(shards), largest / len(shards))
        return jnp.repeat(jnp.exp(steps), dims[axis_at] // shards_of).reshape((-1,) + (1,) * (len(dims) - axis_at - 1))

    gain = one(*shards[0])
    for cut in shards[1:]:
        gain = gain * one(*cut)
    return gain


def gaussian(own_key, shape, deviation, limit, shards=(), held_as=jnp.bfloat16):
    values = deviation * jax.random.normal(own_key, shape, jnp.float32)
    if shards:
        values = values * block_scale(own_key, shape, shards, -0.22, 0.18)
    return jnp.clip(values, -limit, limit).astype(held_as)


def setup_inputs(seed: int = 0) -> dict:
    splits = jax.random.split(jax.random.key(seed), 7)
    return {
        "user_factors": gaussian(splits[0], (USERS, K), 0.21, 1.3, ((0, 32),), jnp.float32),
        "item_factors": gaussian(splits[1], (ITEMS, K), 0.21, 1.3, ((0, 32),), jnp.float32),
        "ratings": gaussian(splits[2], (SUBS, N_ROWS * N_STRATA * ENTRIES), 1.0, 6.0, ((1, 32),), jnp.float32),
        "user_offsets": draw_user_offsets(jax.random.fold_in(splits[6], 71), 0),
        "item_offsets": with_ends(jax.random.randint(splits[4], (SUBS, N_ROWS * N_STRATA * ENTRIES), 0, TILE_COLS), jax.random.fold_in(splits[4], 1), 0, TILE_COLS - 1).astype(jnp.int32),
        "counts": draw_counts(jax.random.fold_in(splits[6], 71), 0),
    }


def reference(user_factors, item_factors, ratings, user_offsets, item_offsets, counts):
    device_count = N_ROWS * N_STRATA
    user_block = USER_DEV * N_STRATA
    user_table = user_factors
    item_table = item_factors
    for sub_epoch in range(SUBS):
        def tile_step(totals, device):
            grad_u, grad_v = totals
            row_pos = device // N_STRATA
            strat_pos = device % N_STRATA
            col_block = ((row_pos - sub_epoch) % N_ROWS) * N_STRATA + strat_pos
            first_slot = (device * ENTRIES).astype(jnp.int32)
            user_index = row_pos * user_block + lax.dynamic_slice_in_dim(user_offsets[sub_epoch], first_slot, ENTRIES)
            item_index = col_block * TILE_COLS + lax.dynamic_slice_in_dim(item_offsets[sub_epoch], first_slot, ENTRIES)
            observed = lax.dynamic_slice_in_dim(ratings[sub_epoch], first_slot, ENTRIES)
            active_mask = (jnp.arange(ENTRIES, dtype=jnp.int32) < counts[sub_epoch, device]).astype(jnp.float32)
            u_rows = user_table[user_index]
            v_rows = item_table[item_index]
            errors = active_mask * (observed - jnp.sum(u_rows * v_rows, axis=1))
            grad_u = grad_u.at[user_index].add(errors[:, None] * v_rows)
            grad_v = grad_v.at[item_index].add(errors[:, None] * u_rows)
            return (grad_u, grad_v), None

        start = (jnp.zeros_like(user_table), jnp.zeros_like(item_table))
        (grad_u, grad_v), _ = lax.scan(tile_step, start, jnp.arange(device_count, dtype=jnp.int32))
        step_size = 0.04 / (1.0 + 0.5 * sub_epoch)
        user_table = user_table + step_size * (grad_u - 0.1 * user_table)
        item_table = item_table + step_size * (grad_v - 0.1 * item_table)
    return user_table, item_table
```

```python
import functools

import jax
import jax.numpy as jnp
from jax import lax
from jax.experimental import pallas as pl
from jax.experimental.pallas import tpu as pltpu
from jax.sharding import PartitionSpec as P

TOUCHED = 32
WHOLE = (0, 1, 2)

F32 = jnp.float32
BF16 = jnp.bfloat16

NN = (((1,), (0,)), ((), ()))
NT = (((1,), (1,)), ((), ()))
TN = (((0,), (0,)), ((), ()))


def dot(a, b, dims):
    return lax.dot_general(a, b, dims, preferred_element_type=F32)


def split2(x):
    hi = x.astype(BF16)
    return hi, (x - hi.astype(F32)).astype(BF16)


def split3(x):
    hi = x.astype(BF16)
    rest = x - hi.astype(F32)
    mid = rest.astype(BF16)
    return hi, mid, (rest - mid.astype(F32)).astype(BF16)


def pick(selector, x, dims):
    hi, mid, lo = split3(x)
    return (dot(selector, hi, dims) + dot(selector, mid, dims)) + dot(selector, lo, dims)


def iota(shape, dim):
    return lax.broadcasted_iota(jnp.int32, shape, dim)


def one_hot(names, rows):
    return (iota((rows, names.shape[1]), 0) == names).astype(F32).astype(BF16)


def run_selector(hot):
    run, entries = hot.shape
    counted = dot(jnp.ones((8, entries), BF16), hot, NT)
    present = (counted > 0).astype(F32)
    before = (iota((run, run), 0) < iota((run, run), 1)).astype(F32).astype(BF16)
    rank = dot(present.astype(BF16), before, NN)
    wanted = iota((TOUCHED, run), 0).astype(F32)
    return ((rank[:1] == wanted).astype(F32) * present[:1]).astype(BF16)


def call(kernel, outs, *args, smem=(), flops=0):
    in_specs = [
        pl.BlockSpec(memory_space=pltpu.SMEM if at in smem else pltpu.VMEM) for at in range(len(args))
    ]
    size = sum(a.size * a.dtype.itemsize for a in args) + sum(o.size * o.dtype.itemsize for o in outs)
    return pl.pallas_call(
        kernel,
        out_shape=list(outs),
        in_specs=in_specs,
        out_specs=[pl.BlockSpec(memory_space=pltpu.VMEM)] * len(outs),
        compiler_params=pltpu.CompilerParams(vmem_limit_bytes=24 * 2**20),
        cost_estimate=pl.CostEstimate(flops=flops, bytes_accessed=size, transcendentals=0),
    )(*args)


def shaped(shape, dtype=F32):
    return jax.ShapeDtypeStruct(shape, dtype)


def pack_kernel(run, at_ref, user_ref, item_ref, rating_ref, count_ref, *out_refs):
    me = at_ref[0, 0]
    for t, out_ref in enumerate(out_refs):
        users = user_ref[t : t + 1, :]
        group = lax.div(users, run)
        users = (group ^ me) * run + (users - group * run)
        active = (iota(users.shape, 1) < count_ref[t, 0]).astype(F32)
        out_ref[0:1, :] = users.astype(F32)
        out_ref[1:2, :] = item_ref[t : t + 1, :].astype(F32)
        out_ref[2:3, :] = rating_ref[t : t + 1, :]
        out_ref[3:4, :] = active


def prep_kernel(run, entry_ref, sel_ref, n_ref, r_ref):
    users = entry_ref[0:1, :].astype(jnp.int32)
    items = entry_ref[1:2, :].astype(jnp.int32)
    active = entry_ref[3:4, :]
    values = split3(entry_ref[2:3, :] * active)
    weights = [active] + [v.astype(F32) for v in values]
    touched = sel_ref.shape[0]
    hots = []
    for k in range(touched // TOUCHED):
        hot = one_hot(users - k * run, run)
        sel = run_selector(hot)
        sel_ref[k * TOUCHED : (k + 1) * TOUCHED, :] = sel
        hots.append(dot(sel, hot, NN))
    hots = jnp.concatenate(hots, axis=0)
    left = jnp.concatenate([(hots * w).astype(BF16) for w in weights], axis=0)
    table = dot(left, one_hot(items, n_ref.shape[1]), NT)
    n_ref[...] = table[:touched]
    r_ref[...] = (table[touched : 2 * touched] + table[2 * touched : 3 * touched]) + table[3 * touched :]


def owner_selector(names, me, run):
    return run_selector(one_hot(names - me * run, run))


def first_rows_kernel(run, at_ref, names_ref, own_ref, out_ref):
    out_ref[...] = pick(owner_selector(names_ref[0:1, :], at_ref[0, 0], run), own_ref[...], NN)


def selectors_kernel(run, n, at_ref, *refs):
    names, outs = refs[:n], refs[n:]
    for t, out_ref in enumerate(outs):
        for k in range(n):
            out_ref[k * TOUCHED : (k + 1) * TOUCHED, :] = owner_selector(names[k][t : t + 1, :], at_ref[0, 0], run)


def tile_kernel(n, whole, *refs):
    rows, refs = refs[:n], refs[n:]
    if whole:
        sel_ref, refs = refs[0], refs[1:]
    n_ref, r_ref, v_ref = refs[:3]
    outs, (uh_ref, ul_ref, wh_ref, wl_ref) = refs[3 : 3 + n], refs[3 + n :]
    for k in range(n):
        part = slice(k * TOUCHED, (k + 1) * TOUCHED)
        hi, lo = split2(rows[k][...])
        if k in whole:
            sel = sel_ref[part, :]
            hi, lo = dot(sel, hi, NN).astype(BF16), dot(sel, lo, NN).astype(BF16)
        uh_ref[part, :] = hi
        ul_ref[part, :] = lo
    uh, ul = uh_ref[...], ul_ref[...]
    vh, vl = split2(v_ref[...])
    products = dot(uh, vh, NT) + (dot(ul, vh, NT) + dot(uh, vl, NT))
    wh, wl = split2(r_ref[...] - n_ref[...] * products)
    wh_ref[...] = wh
    wl_ref[...] = wl
    grads = dot(wh, vh, NN) + (dot(wl, vh, NN) + dot(wh, vl, NN))
    for k in range(n):
        outs[k][...] = grads[k * TOUCHED : (k + 1) * TOUCHED]


def items_kernel(step, uh_ref, ul_ref, wh_ref, wl_ref, v_ref, out_ref):
    uh, ul, wh, wl = uh_ref[...], ul_ref[...], wh_ref[...], wl_ref[...]
    grads = dot(wh, uh, TN) + (dot(wl, uh, TN) + dot(wh, ul, TN))
    v = v_ref[...]
    out_ref[...] = v + step * (grads - 0.1 * v)


def owner_kernel(n, step, *refs):
    parts, (sel_ref, own_ref), refs = refs[:n], refs[n : n + 2], refs[n + 2 :]
    grads = pick(sel_ref[...], jnp.concatenate([part[...] for part in parts], axis=0), TN)
    own = own_ref[...]
    own = own + step * (grads - 0.1 * own)
    if len(refs) == 1:
        refs[0][...] = own
        return
    next_ref, out_ref, outs = refs[0], refs[1], refs[2:]
    out_ref[...] = own
    rows = pick(next_ref[...], own, NN)
    for k in range(n):
        outs[k][...] = rows[k * TOUCHED : (k + 1) * TOUCHED]


def on_device(user_factors, item_factors, ratings, user_offsets, item_offsets, counts):
    n, row_count = lax.axis_size("strata"), lax.axis_size("rows")
    run, rank = user_factors.shape
    items = item_factors.shape[0]
    subs, entries = ratings.shape
    touched = n * TOUCHED
    me = lax.axis_index("strata").astype(jnp.int32).reshape(1, 1)

    def exchange(value, k, shift=0):
        pairs = [
            (r * n + s, ((r + shift) % row_count) * n + (s ^ k)) for r in range(row_count) for s in range(n)
        ]
        if k == 0 and shift == 0:
            return value
        return lax.ppermute(value, ("rows", "strata"), pairs)

    whole = tuple(k for k in WHOLE if k < n)
    names = [None] * n
    names[0] = user_offsets
    for k in range(n):
        if k not in whole:
            names[k] = exchange(user_offsets, k)
    rows = [None] * n
    for k in whole:
        rows[k] = exchange(user_factors, k)
    for k in range(n):
        if k not in whole:
            mine = call(
                functools.partial(first_rows_kernel, run), [shaped((TOUCHED, rank))],
                me, names[k], user_factors, smem=(0,),
            )[0]
            rows[k] = exchange(mine, k)
    for k in whole[1:]:
        names[k] = exchange(user_offsets, k)

    packed = call(
        functools.partial(pack_kernel, run), [shaped((4, entries))] * subs,
        me, user_offsets, item_offsets, ratings, counts, smem=(0, 4),
    )
    selectors = call(
        functools.partial(selectors_kernel, run, n), [shaped((touched, run), BF16)] * subs,
        me, *names, smem=(0,),
    )

    own, block = user_factors, item_factors
    for t in range(subs):
        step = 0.04 / (1.0 + 0.5 * t)
        here = packed[t] if t == 0 else exchange(packed[t], 0, -t)
        sel, n_table, r_table = call(
            functools.partial(prep_kernel, run),
            [shaped((touched, run), BF16), shaped((touched, items)), shaped((touched, items))],
            here, flops=8 * touched * entries * items,
        )
        now_whole = whole if t == 0 else ()
        outs = call(
            functools.partial(tile_kernel, n, now_whole),
            [shaped((TOUCHED, rank))] * n + [shaped((touched, rank), BF16)] * 2 + [shaped((touched, items), BF16)] * 2,
            *rows, *([sel] if now_whole else []), n_table, r_table, block, flops=12 * touched * rank * items,
        )
        grads, saved = outs[:n], outs[n:]
        parts = [exchange(grads[k], k, t) for k in range(n)]
        block = call(
            functools.partial(items_kernel, step), [shaped(block.shape)], *saved, block,
            flops=6 * touched * rank * items,
        )[0]
        if t + 1 < subs:
            own, *mine = call(
                functools.partial(owner_kernel, n, step), [shaped(own.shape)] + [shaped((TOUCHED, rank))] * n,
                *parts, selectors[t], own, selectors[t + 1], flops=12 * touched * rank * run,
            )
            rows = [exchange(mine[k], k, -(t + 1)) for k in range(n)]
        else:
            own = call(
                functools.partial(owner_kernel, n, step), [shaped(own.shape)],
                *parts, selectors[t], own, flops=6 * touched * rank * run,
            )[0]
    return own, block


def solution(mesh):
    return jax.shard_map(
        on_device,
        mesh=mesh,
        in_specs=(
            P(("rows", "strata"), None),
            P(("rows", "strata"), None),
            P(None, ("rows", "strata")),
            P(None, ("rows", "strata")),
            P(None, ("rows", "strata")),
            P(None, ("rows", "strata")),
        ),
        out_specs=(P(("rows", "strata"), None), P(("rows", "strata"), None)),
        check_vma=False,
    )
```

```python
import functools

import jax
import jax.numpy as jnp
from jax import lax
from jax.experimental import pallas as pl
from jax.experimental.pallas import tpu as pltpu
from jax.sharding import PartitionSpec as P

TOUCHED = 32
WHOLE = (0, 1, 2)


def first_pieces(n, whole):
    rest = tuple(k for k in range(n) if k not in whole)
    return (whole, rest) if rest else (whole,)


def later_pieces(n):
    order = (0, *range(n - 1, 0, -1))
    return (order[: n // 2], order[n // 2 :])


F32 = jnp.float32
BF16 = jnp.bfloat16
LANES = 128
FIELDS = 3
FIRST_FLOPS = 10**11
SPLIT_FLOPS = 0
PACK_FLOPS = 10**8
PREP_FLOPS = 10**8
TILE_FLOPS = 10**9

NN = (((1,), (0,)), ((), ()))
NT = (((1,), (1,)), ((), ()))
TN = (((0,), (0,)), ((), ()))


def dot(a, b, dims):
    return lax.dot_general(a, b, dims, preferred_element_type=F32)


def split2(x):
    hi = x.astype(BF16)
    return hi, (x - hi.astype(F32)).astype(BF16)


def split3(x):
    hi = x.astype(BF16)
    rest = x - hi.astype(F32)
    mid = rest.astype(BF16)
    return hi, mid, (rest - mid.astype(F32)).astype(BF16)


def pick(selector, x, dims):
    hi, mid, lo = split3(x)
    return (dot(selector, hi, dims) + dot(selector, mid, dims)) + dot(selector, lo, dims)


def iota(shape, dim):
    return lax.broadcasted_iota(jnp.int32, shape, dim)


def one_hot(names, rows):
    return (iota((rows, names.shape[1]), 0) == names).astype(F32).astype(BF16)


def touched_by(names):
    def present(run):
        hot = iota((run, names.shape[1]), 0) == names
        return jnp.max(jnp.where(hot, 1.0, 0.0), axis=1, keepdims=True)

    return present


def ranks(present):
    run = present.shape[0]
    before = (iota((run, run), 0) > iota((run, run), 1)).astype(F32).astype(BF16)
    return jnp.where(present > 0.0, dot(before, present.astype(BF16), NN), -1.0)


def selector(rank):
    return (iota((TOUCHED, rank.shape[1]), 0).astype(F32) == rank).astype(F32).astype(BF16)


def call(kernel, outs, *args, smem=(), hbm=(), scratch=(), flops=0):
    def space(at):
        return pltpu.SMEM if at in smem else pltpu.HBM if at in hbm else pltpu.VMEM

    in_specs = [pl.BlockSpec(memory_space=space(at)) for at in range(len(args))]
    size = sum(a.size * a.dtype.itemsize for a in (*args, *outs)) if flops else 0
    return pl.pallas_call(
        kernel,
        out_shape=list(outs),
        in_specs=[pl.BlockSpec(memory_space=pltpu.VMEM)] * len(args),
        out_specs=[pl.BlockSpec(memory_space=pltpu.VMEM)] * len(outs),
        compiler_params=pltpu.CompilerParams(vmem_limit_bytes=24 * 2**20),
        cost_estimate=pl.CostEstimate(flops=flops, bytes_accessed=size, transcendentals=0),
    )(*args)


def shaped(shape, dtype=F32):
    return jax.ShapeDtypeStruct(shape, dtype)


def split_kernel(own_ref, *out_refs):
    for out_ref, part in zip(out_refs, split3(own_ref[...])):
        out_ref[...] = part


def first_rows_kernel(names_ref, *refs):
    *part_refs, out_ref = refs
    run = part_refs[0].shape[0]
    present = touched_by(names_ref[0:1, :] - lax.axis_index("strata") * run)(run)
    rank = ranks(jnp.broadcast_to(present, (run, LANES)))[:, :TOUCHED]
    sel = (iota(rank.shape, 1).astype(F32) == rank).astype(F32).astype(BF16)
    hi, mid, lo = [dot(sel, ref[...], TN) for ref in part_refs]
    out_ref[...] = (hi + mid) + lo


def run_names(user_ref, t, k, run):
    return user_ref[t : t + 1, :] - (lax.axis_index("strata") ^ k) * run


def pack_entries(n, t, user_ref, item_ref, rating_ref, count_ref, rank, out_ref):
    run = rank.shape[0]
    compact = jnp.zeros((1, user_ref.shape[1]), F32)
    for k in range(n):
        hot = iota((run, user_ref.shape[1]), 0) == run_names(user_ref, t, k, run)
        value = rank[:, t * n + k : t * n + k + 1] + float(k * TOUCHED)
        compact = compact + jnp.sum(jnp.where(hot, value, 0.0), axis=0, keepdims=True)
    active = iota(compact.shape, 1) < count_ref[t : t + 1, 0:1]
    out_ref[0:1, :] = jnp.where(active, compact, -1.0)
    out_ref[1:2, :] = item_ref[t : t + 1, :].astype(F32)
    out_ref[2:3, :] = rating_ref[t : t + 1, :]


def pack_first_kernel(n, user_ref, item_ref, rating_ref, count_ref, rank_ref, codes_ref, out_ref):
    run, width = rank_ref.shape
    lane = iota((run, width), 1)
    present = jnp.zeros((run, width), F32)
    for t in range(user_ref.shape[0]):
        for k in range(n):
            named = touched_by(run_names(user_ref, t, k, run))(run)
            present = jnp.where(lane == t * n + k, named, present)
    rank = ranks(present)
    rank_ref[...] = rank
    codes_ref[...] = rank.T[: codes_ref.shape[0]]
    pack_entries(n, 0, user_ref, item_ref, rating_ref, count_ref, rank, out_ref)


def pack_kernel(n, user_ref, item_ref, rating_ref, count_ref, rank_ref, *out_refs):
    for t, out_ref in enumerate(out_refs, 1):
        pack_entries(n, t, user_ref, item_ref, rating_ref, count_ref, rank_ref[...], out_ref)


def prep_kernel(entry_ref, n_ref, r_ref):
    touched, items = n_ref.shape
    per = max((entry_ref.shape[0] - TOUCHED) // FIELDS, 1)
    lines = [entry_ref[at : at + 1, :] for at in range(entry_ref.shape[0] - FIELDS * per, entry_ref.shape[0])]
    fields = [jnp.concatenate(lines[f * per : (f + 1) * per], axis=1) for f in range(FIELDS)]
    users = fields[0].astype(jnp.int32)
    hot = (iota((touched, users.shape[1]), 0) == users).astype(F32)
    values = split3(fields[2])
    left = [hot.astype(BF16)] + [(hot * v.astype(F32)).astype(BF16) for v in values]
    table = dot(jnp.concatenate(left, axis=0), one_hot(fields[1].astype(jnp.int32), items), NT)
    n_ref[...] = table[:touched]
    r_ref[...] = (table[touched : 2 * touched] + table[2 * touched : 3 * touched]) + table[3 * touched :]


def twice(ah, al, bh, bl, dims):
    both = dot(jnp.concatenate([ah, al], axis=0), bh, dims)
    rows = ah.shape[0]
    return (both[:rows] + both[rows:]) + dot(ah, bl, dims)


def tile_kernel(piece, whole, first, *refs):
    rows, refs = refs[: len(piece)], refs[len(piece) :]
    if first:
        (codes_ref, low_ref), refs = refs[:2], refs[2:]
    parts = 1 if first and 0 in piece else 2
    v_refs, (n_ref, r_ref), refs = refs[:parts], refs[parts : parts + 2], refs[parts + 2 :]
    outs, (uh_ref, ul_ref, wh_ref, wl_ref), v_outs = refs[: len(piece)], refs[len(piece) :][:4], refs[len(piece) + 4 :]
    if v_outs:
        vh, vl = split2(v_refs[0][...])
        v_outs[0][...] = vh
        v_outs[1][...] = vl
    else:
        vh, vl = v_refs[0][...], v_refs[1][...]
    tables = ([], [])
    for at, k in enumerate(piece):
        if first and k == 0:
            hi, lo = rows[at][...], low_ref[...]
        else:
            hi, lo = split2(rows[at][...] if k in whole else rows[at][:TOUCHED, :])
        if k in whole:
            sel = selector(codes_ref[k : k + 1, :])
            hi, lo = dot(sel, hi, NN).astype(BF16), dot(sel, lo, NN).astype(BF16)
        part = slice(at * TOUCHED, (at + 1) * TOUCHED)
        uh_ref[part, :] = hi
        ul_ref[part, :] = lo
        for table, ref in zip(tables, (n_ref, r_ref)):
            table.append(ref[k * TOUCHED : (k + 1) * TOUCHED, :])
    n_table, r_table = [jnp.concatenate(table, axis=0) for table in tables]
    uh, ul = uh_ref[...], ul_ref[...]
    wh, wl = split2(r_table - n_table * twice(uh, ul, vh, vl, NT))
    wh_ref[...] = wh
    wl_ref[...] = wl
    grads = twice(wh, wl, vh, vl, NN)
    for at, k in enumerate(piece):
        outs[at][:TOUCHED, :] = grads[at * TOUCHED : (at + 1) * TOUCHED]
        if first:
            run = codes_ref.shape[1]
            outs[at][TOUCHED:, :] = jnp.zeros((outs[at].shape[0] - TOUCHED, outs[at].shape[1]), F32)
            n = n_ref.shape[0] // TOUCHED
            for t in range(codes_ref.shape[0] // n):
                outs[at][TOUCHED + t : TOUCHED + t + 1, :run] = codes_ref[t * n + k : t * n + k + 1, :]


def items_kernel(step, count, *refs):
    uh, ul, wh, wl = [jnp.concatenate([refs[4 * at + i][...] for at in range(count)], axis=0) for i in range(4)]
    v_ref, out_ref, *part_refs = refs[4 * count :]
    grads = dot(wh, uh, TN) + (dot(wl, uh, TN) + dot(wh, ul, TN))
    v = v_ref[...]
    v = v + step * (grads - 0.1 * v)
    out_ref[...] = v
    if part_refs:
        part_refs[0][...], part_refs[1][...] = split2(v)


def owner_kernel(n, t, step, entry_rows, *refs):
    parts, refs = refs[:n], refs[n:]
    if t == 0:
        ranked = parts
    else:
        ranked, refs = refs[:n], refs[n:]
    if entry_rows:
        entry_ref, refs = refs[0], refs[1:]
    own_ref, out_ref, outs = refs[0], refs[1], refs[2:]
    run = own_ref.shape[0]

    def selectors(sub):
        at = slice(TOUCHED + sub, TOUCHED + sub + 1)
        return jnp.concatenate([selector(ref[at, :run]) for ref in ranked], axis=0)

    grads = pick(selectors(t), jnp.concatenate([part[:TOUCHED, :] for part in parts], axis=0), TN)
    own = own_ref[...]
    own = own + step * (grads - 0.1 * own)
    out_ref[...] = own
    if outs:
        rows = pick(selectors(t + 1), own, NN)
        for k in range(n):
            outs[k][:TOUCHED, :] = rows[k * TOUCHED : (k + 1) * TOUCHED]
        per, width = entry_rows // FIELDS, own_ref.shape[1]
        for f in range(FIELDS):
            for at in range(per):
                low = TOUCHED + f * per + at
                outs[0][low : low + 1, :] = entry_ref[f : f + 1, at * width : (at + 1) * width]


def on_device(user_factors, item_factors, ratings, user_offsets, item_offsets, counts):
    n, row_count = lax.axis_size("strata"), lax.axis_size("rows")
    run, rank = user_factors.shape
    items = item_factors.shape[0]
    subs, entries = ratings.shape
    touched = n * TOUCHED
    entry_rows = FIELDS * (entries // rank)
    ranked_rows = TOUCHED + -(-subs // 8) * 8

    def exchange(value, k, shift=0):
        if k == 0 and shift == 0:
            return value
        pairs = [
            (r * n + s, ((r + shift) % row_count) * n + (s ^ k)) for r in range(row_count) for s in range(n)
        ]
        return lax.ppermute(value, ("rows", "strata"), pairs)

    whole = tuple(k for k in WHOLE if k < n)
    pieces = call(split_kernel, [shaped((run, rank), BF16)] * 3, user_factors, flops=SPLIT_FLOPS)
    rows = [pieces[0]] + [None] * (n - 1)
    for k in range(n):
        if k in whole:
            rows[k] = exchange(user_factors, k)
        elif k:
            mine = call(
                first_rows_kernel, [shaped((TOUCHED, rank))], exchange(user_offsets, k), *pieces,
                flops=FIRST_FLOPS,
            )[0]
            rows[k] = exchange(mine, k)

    listed = (user_offsets, item_offsets, ratings, counts)
    if len(whole) < n:
        listed, mine = lax.optimization_barrier((listed, mine))
    width = -(-subs * n // LANES) * LANES
    ranked, codes, packed = call(
        functools.partial(pack_first_kernel, n),
        [shaped((run, width)), shaped((subs * n, run)), shaped((FIELDS, entries))],
        *listed, flops=PACK_FLOPS,
    )

    own, block = user_factors, item_factors
    block_parts = None
    for t in range(subs):
        step = 0.04 / (1.0 + 0.5 * t)
        first, last = t == 0, t + 1 == subs
        n_table, r_table = call(
            prep_kernel, [shaped((touched, items))] * 2, packed if first else rows[0], flops=PREP_FLOPS,
        )
        height = ranked_rows if first else TOUCHED
        parts, saved = [None] * n, []
        for piece in first_pieces(n, whole) if first else later_pieces(n):
            splits = first and 0 in piece
            size = len(piece) * TOUCHED
            outs = call(
                functools.partial(tile_kernel, piece, whole if first else (), first),
                [shaped((height, rank))] * len(piece) + [shaped((size, rank), BF16)] * 2
                + [shaped((size, items), BF16)] * 2 + [shaped(block.shape, BF16)] * (2 * splits),
                *[rows[k] for k in piece], *([codes, pieces[1]] if first else []),
                *([block] if splits else block_parts), n_table, r_table, flops=TILE_FLOPS,
            )
            for k, grads in zip(piece, outs):
                parts[k] = exchange(grads, k, t)
            saved += outs[len(piece) :][:4]
            if splits:
                block_parts = outs[len(piece) + 4 :]
        block, *block_parts = call(
            functools.partial(items_kernel, step, len(saved) // 4),
            [shaped(block.shape)] + ([] if last else [shaped(block.shape, BF16)] * 2),
            *saved, block, flops=6 * touched * rank * items,
        )
        if not last:
            parts, block, block_parts = lax.optimization_barrier((parts, block, block_parts))
        if first:
            codes_parts = parts
            if not last:
                ranked = lax.optimization_barrier((ranked, saved[0]))[0]
                later = call(
                    functools.partial(pack_kernel, n), [shaped((FIELDS, entries))] * (subs - 1),
                    *listed, ranked, flops=PACK_FLOPS,
                )
        own, *mine = call(
            functools.partial(owner_kernel, n, t, step, 0 if last else entry_rows),
            [shaped(own.shape)] + ([] if last else [shaped((TOUCHED + (k == 0) * entry_rows, rank)) for k in range(n)]),
            *parts, *([] if first else codes_parts), *([] if last else [later[t]]), own, flops=12 * touched * rank * run,
        )
        if not last:
            rows = [None] * n
            for k in (k for piece in later_pieces(n) for k in piece):
                rows[k] = exchange(mine[k], k, -(t + 1))
    return own, block


def solution(mesh):
    return jax.shard_map(
        on_device,
        mesh=mesh,
        in_specs=(
            P(("rows", "strata"), None),
            P(("rows", "strata"), None),
            P(None, ("rows", "strata")),
            P(None, ("rows", "strata")),
            P(None, ("rows", "strata")),
            P(None, ("rows", "strata")),
        ),
        out_specs=(P(("rows", "strata"), None), P(("rows", "strata"), None)),
        check_vma=False,
    )
```

```python
import functools

import jax
import jax.numpy as jnp
from jax import lax
from jax.experimental import pallas as pl
from jax.experimental.pallas import tpu as pltpu
from jax.sharding import PartitionSpec as P

TOUCHED = 32
WHOLE = (0, 1, 2)


BLOCK_LATE = 0
STACK_LATE = False
VMEM = 24
PACK_LATE = True
HOME_CHUNKS = 4
FIN_LATE = True
FLOPS = dict(
    split=80000000, first=100000000000, pack=1400000000, prep0=900000000, block=200000000, tile0=1000000000, tile1=800000000, items=900000000, pack1=500000000,
    prep1=900000000, stack=0, next=900000000, owner=6000000000, join=0, preph=900000000, home=2000000000, fin=1200000000,
)

F32 = jnp.float32
BF16 = jnp.bfloat16
LANES = 128
FIELDS = 3

NN = (((1,), (0,)), ((), ()))
NT = (((1,), (1,)), ((), ()))
TN = (((0,), (0,)), ((), ()))


def dot(a, b, dims):
    return lax.dot_general(a, b, dims, preferred_element_type=F32)


def split2(x):
    hi = x.astype(BF16)
    return hi, (x - hi.astype(F32)).astype(BF16)


def split3(x):
    hi = x.astype(BF16)
    rest = x - hi.astype(F32)
    mid = rest.astype(BF16)
    return hi, mid, (rest - mid.astype(F32)).astype(BF16)


def pick(selector, x, dims):
    hi, mid, lo = split3(x)
    return (dot(selector, hi, dims) + dot(selector, mid, dims)) + dot(selector, lo, dims)


def iota(shape, dim):
    return lax.broadcasted_iota(jnp.int32, shape, dim)


def one_hot(names, rows):
    return (iota((rows, names.shape[1]), 0) == names).astype(F32).astype(BF16)


def touched_by(names):
    def present(run):
        hot = iota((run, names.shape[1]), 0) == names
        return jnp.max(jnp.where(hot, 1.0, 0.0), axis=1, keepdims=True)

    return present


def ranks(present):
    run = present.shape[0]
    before = (iota((run, run), 0) > iota((run, run), 1)).astype(F32).astype(BF16)
    return jnp.where(present > 0.0, dot(before, present.astype(BF16), NN), -1.0)


def selector(rank):
    return (iota((TOUCHED, rank.shape[1]), 0).astype(F32) == rank).astype(F32).astype(BF16)


def call(kernel, outs, *args, flops=0, after=(), hbm_out=False, scratch=()):
    size = sum(a.size * a.dtype.itemsize for a in (*args, *outs)) if flops else 0

    def body(*refs):
        kernel(*refs[: len(args)], *refs[len(args) + len(after) :])

    return pl.pallas_call(
        body,
        out_shape=list(outs),
        in_specs=[pl.BlockSpec(memory_space=pltpu.VMEM)] * len(args) + [pl.BlockSpec(memory_space=pl.ANY)] * len(after),
        out_specs=[pl.BlockSpec(memory_space=pl.ANY if hbm_out and at == 0 else pltpu.VMEM) for at in range(len(outs))],
        scratch_shapes=list(scratch),
        compiler_params=pltpu.CompilerParams(vmem_limit_bytes=VMEM * 2**20),
        cost_estimate=pl.CostEstimate(flops=flops, bytes_accessed=size, transcendentals=0),
    )(*args, *after)


def shaped(shape, dtype=F32):
    return jax.ShapeDtypeStruct(shape, dtype)


def split_kernel(own_ref, *out_refs):
    for out_ref, part in zip(out_refs, split3(own_ref[...])):
        out_ref[...] = part


def first_rows_kernel(names_ref, *refs):
    *part_refs, out_ref = refs
    run = part_refs[0].shape[0]
    present = touched_by(names_ref[0:1, :] - lax.axis_index("strata") * run)(run)
    rank = ranks(jnp.broadcast_to(present, (run, LANES)))[:, :TOUCHED]
    sel = (iota(rank.shape, 1).astype(F32) == rank).astype(F32).astype(BF16)
    hi, mid, lo = [dot(sel, ref[...], TN) for ref in part_refs]
    out_ref[...] = (hi + mid) + lo


def run_names(user_ref, t, k, run):
    return user_ref[t : t + 1, :] - (lax.axis_index("strata") ^ k) * run


def pack_entries(n, t, user_ref, item_ref, rating_ref, count_ref, rank, out_ref):
    run = rank.shape[0]
    compact = jnp.zeros((1, user_ref.shape[1]), F32)
    for k in range(n):
        hot = iota((run, user_ref.shape[1]), 0) == run_names(user_ref, t, k, run)
        value = rank[:, t * n + k : t * n + k + 1] + float(k * TOUCHED)
        compact = compact + jnp.sum(jnp.where(hot, value, 0.0), axis=0, keepdims=True)
    active = iota(compact.shape, 1) < count_ref[0:1, t : t + 1]
    out_ref[0:1, :] = jnp.where(active, compact, -1.0)
    out_ref[1:2, :] = item_ref[t : t + 1, :].astype(F32)
    out_ref[2:3, :] = rating_ref[t : t + 1, :]


def pack_first_kernel(n, user_ref, item_ref, rating_ref, count_ref, rank_ref, codes_ref, out_ref):
    run, width = rank_ref.shape
    lane = iota((run, width), 1)
    present = jnp.zeros((run, width), F32)
    for t in range(user_ref.shape[0]):
        for k in range(n):
            named = touched_by(run_names(user_ref, t, k, run))(run)
            present = jnp.where(lane == t * n + k, named, present)
    rank = ranks(present)
    rank_ref[...] = rank
    codes_ref[...] = rank.T[: codes_ref.shape[0]]
    pack_entries(n, 0, user_ref, item_ref, rating_ref, count_ref, rank, out_ref)


def pack_kernel(n, t, user_ref, item_ref, rating_ref, count_ref, rank_ref, out_ref):
    pack_entries(n, t, user_ref, item_ref, rating_ref, count_ref, rank_ref[...], out_ref)


def block_kernel(v_ref, vh_ref, vl_ref):
    vh_ref[...], vl_ref[...] = split2(v_ref[...])


def prep_kernel(entry_ref, n_ref, r_ref):
    touched, items = n_ref.shape
    low = touched if entry_ref.shape[0] > touched else 0
    per = (entry_ref.shape[0] - low) // FIELDS
    fields = [
        jnp.concatenate([entry_ref[at : at + 1, :] for at in range(low + f * per, low + (f + 1) * per)], axis=1)
        for f in range(FIELDS)
    ]
    users = fields[0].astype(jnp.int32)
    hot = (iota((touched, users.shape[1]), 0) == users).astype(F32)
    values = split3(fields[2])
    left = [hot.astype(BF16)] + [(hot * v.astype(F32)).astype(BF16) for v in values]
    table = dot(jnp.concatenate(left, axis=0), one_hot(fields[1].astype(jnp.int32), items), NT)
    n_ref[...] = table[:touched]
    r_ref[...] = (table[touched : 2 * touched] + table[2 * touched : 3 * touched]) + table[3 * touched :]


def twice(ah, al, bh, bl, dims):
    both = dot(jnp.concatenate([ah, al], axis=0), bh, dims)
    rows = ah.shape[0]
    return (both[:rows] + both[rows:]) + dot(ah, bl, dims)


def tile_kernel(piece, whole, first, *refs):
    rows, refs = refs[: len(piece)], refs[len(piece) :]
    if first:
        (codes_ref, low_ref), refs = refs[:2], refs[2:]
    (vh_ref, vl_ref, n_ref, r_ref), refs = refs[:4], refs[4:]
    outs, factors_ref = refs[: len(piece)], refs[len(piece)]
    vh, vl = vh_ref[...], vl_ref[...]
    parts = []
    for at, k in enumerate(piece):
        if first and k == 0:
            hi, lo = rows[at][...], low_ref[...]
        else:
            hi, lo = split2(rows[at][...])
        if k in whole:
            sel = selector(codes_ref[k : k + 1, :])
            hi, lo = dot(sel, hi, NN).astype(BF16), dot(sel, lo, NN).astype(BF16)
        parts.append((hi, lo))
    uh, ul = [jnp.concatenate(x, axis=0) for x in zip(*parts)]
    n_table, r_table = [
        jnp.concatenate([ref[k * TOUCHED : (k + 1) * TOUCHED, :] for k in piece], axis=0) for ref in (n_ref, r_ref)
    ]
    weights = r_table - n_table * twice(uh, ul, vh, vl, NT)
    wh, wl = split2(weights)
    grads = twice(wh, wl, vh, vl, NN)
    for at, k in enumerate(piece):
        outs[at][:TOUCHED, :] = grads[at * TOUCHED : (at + 1) * TOUCHED]
        if first:
            run = codes_ref.shape[1]
            outs[at][TOUCHED:, :] = jnp.zeros((outs[at].shape[0] - TOUCHED, outs[at].shape[1]), F32)
            n = n_ref.shape[0] // TOUCHED
            for t in range(codes_ref.shape[0] // n):
                outs[at][TOUCHED + t : TOUCHED + t + 1, :run] = codes_ref[t * n + k : t * n + k + 1, :]
    if first:
        items = weights.shape[1]
        factors_ref[:, :items] = weights
        factors_ref[:, items:] = uh.astype(F32) + ul.astype(F32)


def item_update(step, weights, rows, v):
    (wh, wl), (uh, ul) = split2(weights), split2(rows)
    grads = dot(wh, uh, TN) + (dot(wl, uh, TN) + dot(wh, ul, TN))
    return v + step * (grads - 0.1 * v)


def items_kernel(step, count, *refs):
    factors = jnp.concatenate([ref[...] for ref in refs[:count]], axis=0)
    v_ref, *out_refs = refs[count:]
    v = v_ref[...]
    items = v.shape[0]
    v = item_update(step, factors[:, :items], factors[:, items:], v)
    if len(out_refs) == 3:
        out_refs[0][...] = v
    out_refs[-2][...], out_refs[-1][...] = split2(v)


def home_kernel(step, rows_ref, n_ref, r_ref, v_ref, vh_ref, vl_ref, out_ref, done_ref, held_ref, sems):
    rows = rows_ref[: n_ref.shape[0], :]
    done_ref[...] = jnp.zeros_like(done_ref)
    uh, ul = split2(rows)
    weights = r_ref[...] - n_ref[...] * twice(uh, ul, vh_ref[...], vl_ref[...], NT)
    chunk = held_ref.shape[0] // HOME_CHUNKS
    copies = []
    for at in range(HOME_CHUNKS):
        part = slice(at * chunk, (at + 1) * chunk)
        held_ref[part, :] = item_update(step, weights[:, part], rows, v_ref[part, :])
        copies.append(pltpu.make_async_copy(held_ref.at[part], out_ref.at[part], sems.at[at]))
        copies[-1].start()
    for copy in copies:
        copy.wait()


def join_kernel(*refs):
    *row_refs, entry_ref, out_ref = refs
    at = 0
    for ref in row_refs:
        out_ref[at : at + TOUCHED, :] = ref[...]
        at += TOUCHED
    width = out_ref.shape[1]
    for f in range(entry_ref.shape[0]):
        for low in range(0, entry_ref.shape[1], width):
            out_ref[at : at + 1, :] = entry_ref[f : f + 1, low : low + width]
            at += 1


def stack_kernel(*refs):
    *in_refs, out_ref = refs
    at = 0
    for ref in in_refs:
        out_ref[at : at + ref.shape[0], :] = ref[...]
        at += ref.shape[0]


def owner_kernel(order, t, step, *refs):
    n = len(order)
    parts, refs = refs[:n], refs[n:]
    if t == 0:
        ranked = parts
    else:
        ranked, refs = refs[:n], refs[n:]
    own_ref, out_ref, outs = refs[0], refs[1], refs[2:]
    run = own_ref.shape[0]

    def selectors(sub):
        at = slice(TOUCHED + sub, TOUCHED + sub + 1)
        return jnp.concatenate([selector(ref[at, :run]) for ref in ranked], axis=0)

    grads = pick(selectors(t), jnp.concatenate([part[:TOUCHED, :] for part in parts], axis=0), TN)
    own = own_ref[...]
    own = own + step * (grads - 0.1 * own)
    out_ref[...] = own
    if outs:
        rows = pick(selectors(t + 1), own, NN)
        for at in range(n):
            outs[at][...] = rows[at * TOUCHED : (at + 1) * TOUCHED]


def on_device(user_factors, item_factors, ratings, user_offsets, item_offsets, counts):
    n, row_count = lax.axis_size("strata"), lax.axis_size("rows")
    run, rank = user_factors.shape
    items = item_factors.shape[0]
    subs, entries = ratings.shape
    touched = n * TOUCHED
    ranked_rows = TOUCHED + -(-subs // 8) * 8
    steps = [0.04 / (1.0 + 0.5 * t) for t in range(subs)]
    if subs != 2:
        raise ValueError("two sub-epochs")
    sent = (0, *range(n - 1, 0, -1))
    later_pieces = (sent[: n - n // 4], sent[n - n // 4 :])

    def exchange(value, k, shift=0):
        if k == 0 and shift == 0:
            return value
        pairs = [
            (r * n + s, ((r + shift) % row_count) * n + (s ^ k)) for r in range(row_count) for s in range(n)
        ]
        return lax.ppermute(value, ("rows", "strata"), pairs)

    def prepare(values, flops, after=()):
        return call(prep_kernel, [shaped((touched, items))] * 2, values, flops=flops, after=after)

    def tile(piece, first, *args, after=()):
        *out, factors = call(
            functools.partial(tile_kernel, piece, whole if first else (), first),
            [shaped((ranked_rows if first else TOUCHED, rank))] * len(piece)
            + [shaped((len(piece) * TOUCHED, items + rank) if first else (8, LANES))],
            *[rows[k] for k in piece], *args, flops=FLOPS["tile%d" % (not first)], after=after,
        )
        grads.update(zip(piece, out))
        return factors

    whole = tuple(k for k in WHOLE if k < n)
    pieces = call(split_kernel, [shaped((run, rank), BF16)] * 3, user_factors, flops=FLOPS["split"])
    rows = [pieces[0]] + [None] * (n - 1)
    picked = []
    for k in range(1, n):
        if k in whole:
            rows[k] = exchange(user_factors, k)
        else:
            picked += call(
                first_rows_kernel, [shaped((TOUCHED, rank))], exchange(user_offsets, k), *pieces,
                flops=FLOPS["first"],
            )
            rows[k] = exchange(picked[-1], k)
    listed = (user_offsets, item_offsets, ratings, counts.reshape(1, subs))
    width = -(-subs * n // LANES) * LANES
    ranked, codes, packed = call(
        functools.partial(pack_first_kernel, n),
        [shaped((run, width)), shaped((subs * n, run)), shaped((FIELDS, entries))],
        *listed, flops=FLOPS["pack"], after=picked,
    )
    tables = prepare(packed, FLOPS["prep0"])
    block_parts = call(
        block_kernel, [shaped(item_factors.shape, BF16)] * 2,
        item_factors, flops=FLOPS["block"], after=[*(picked if BLOCK_LATE != 2 else [rows[1]]), *(tables if BLOCK_LATE == 1 else [])],
    )
    next_block = exchange(item_factors, 0, 1)

    grads, factors = {}, []
    rest = tuple(k for k in range(n) if k not in whole)
    for piece in (whole, rest) if rest else (whole,):
        factors.append(tile(piece, True, codes, pieces[1], *block_parts, *tables, after=factors[-1:]))
    parts = [exchange(grads[k], k) for k in range(n)]
    block, *block_parts = call(
        functools.partial(items_kernel, steps[0], len(factors)),
        [shaped(item_factors.shape)] + [shaped(item_factors.shape, BF16)] * 2,
        *factors, item_factors, flops=FLOPS["items"],
    )
    packed = call(
        functools.partial(pack_kernel, n, 1), [shaped((FIELDS, entries))],
        *listed, ranked, flops=FLOPS["pack1"], after=[block] if PACK_LATE else factors[-1:],
    )[0]
    tables = prepare(packed, FLOPS["prep1"])
    factors = call(
        stack_kernel, [shaped((touched, items + rank))], *factors, flops=FLOPS["stack"],
        after=[block] if STACK_LATE else [],
    )[0]
    next_parts = call(
        functools.partial(items_kernel, steps[0], 1), [shaped(item_factors.shape, BF16)] * 2,
        exchange(factors, 0, 1), next_block, flops=FLOPS["next"],
    )
    ranked = [parts[k] for k in sent]
    own, *mine = call(
        functools.partial(owner_kernel, sent, 0, steps[0]),
        [shaped(user_factors.shape)] + [shaped((TOUCHED, rank))] * n,
        *ranked, user_factors, flops=FLOPS["owner"], after=[block, *tables],
    )

    for k, value in zip(sent, mine):
        rows[k] = exchange(value, k)
    grads = {}
    done = []
    for piece in later_pieces:
        done.append(tile(piece, False, *next_parts, *tables, after=done[-1:]))
    parts = [exchange(grads[k], k) for k in range(n)]
    joined = call(
        join_kernel, [shaped((touched + FIELDS * entries // rank, rank))], *rows, packed, flops=FLOPS["join"],
        after=[grads[later_pieces[0][0]]],
    )[0]
    joined = exchange(joined, 0, -1)
    tables_home = prepare(joined, FLOPS["preph"], [grads[later_pieces[-1][0]]])
    block, after_block = call(
        functools.partial(home_kernel, steps[1]), [shaped(block.shape), shaped((8, LANES))],
        joined, *tables_home, block, *block_parts,
        flops=FLOPS["home"], after=[grads[later_pieces[-1][0]]], hbm_out=True,
        scratch=[pltpu.VMEM(block.shape, F32), pltpu.SemaphoreType.DMA((HOME_CHUNKS,))],
    )
    own = call(
        functools.partial(owner_kernel, sent, 1, steps[1]), [shaped(own.shape)],
        *[parts[k] for k in sent], *[dict(zip(sent, ranked))[k] for k in sent], own, flops=FLOPS["fin"],
        after=[after_block] if FIN_LATE else [],
    )[0]
    return own, block


def solution(mesh):
    return jax.shard_map(
        on_device,
        mesh=mesh,
        in_specs=(
            P(("rows", "strata"), None),
            P(("rows", "strata"), None),
            P(None, ("rows", "strata")),
            P(None, ("rows", "strata")),
            P(None, ("rows", "strata")),
            P(None, ("rows", "strata")),
        ),
        out_specs=(P(("rows", "strata"), None), P(("rows", "strata"), None)),
        check_vma=False,
    )
```

```python
import functools

import jax
import jax.numpy as jnp
from jax import lax
from jax.experimental import pallas as pl
from jax.experimental.pallas import tpu as pltpu
from jax.sharding import PartitionSpec as P

TOUCHED = 32
WHOLE = (0, 1, 2)

HOME_CHUNKS = 4
FLOPS = dict(
    split=8 * 10**7, first=10**11, pack=14 * 10**8, prep0=9 * 10**8, block=2 * 10**8, tile0=10**9, tile1=8 * 10**8,
    items=9 * 10**8, pack1=5 * 10**8, prep1=9 * 10**8, stack=0, next=2 * 10**9, owner=6 * 10**9, join=0,
    home=25 * 10**8, fin=12 * 10**8,
)

F32 = jnp.float32
BF16 = jnp.bfloat16
LANES = 128
FIELDS = 3

NN = (((1,), (0,)), ((), ()))
NT = (((1,), (1,)), ((), ()))
TN = (((0,), (0,)), ((), ()))


def dot(a, b, dims):
    return lax.dot_general(a, b, dims, preferred_element_type=F32)


def split2(x):
    hi = x.astype(BF16)
    return hi, (x - hi.astype(F32)).astype(BF16)


def split3(x):
    hi = x.astype(BF16)
    rest = x - hi.astype(F32)
    mid = rest.astype(BF16)
    return hi, mid, (rest - mid.astype(F32)).astype(BF16)


def pick(selector, x, dims):
    hi, mid, lo = split3(x)
    return (dot(selector, hi, dims) + dot(selector, mid, dims)) + dot(selector, lo, dims)


def iota(shape, dim):
    return lax.broadcasted_iota(jnp.int32, shape, dim)


def one_hot(names, rows):
    return (iota((rows, names.shape[1]), 0) == names).astype(F32).astype(BF16)


def touched_by(names):
    def present(run):
        hot = iota((run, names.shape[1]), 0) == names
        return jnp.max(jnp.where(hot, 1.0, 0.0), axis=1, keepdims=True)

    return present


def ranks(present):
    run = present.shape[0]
    before = (iota((run, run), 0) > iota((run, run), 1)).astype(F32).astype(BF16)
    return jnp.where(present > 0.0, dot(before, present.astype(BF16), NN), -1.0)


def selector(rank):
    return (iota((TOUCHED, rank.shape[1]), 0).astype(F32) == rank).astype(F32).astype(BF16)


def call(kernel, outs, *args, flops=0, after=(), hbm_out=False, scratch=()):
    size = sum(a.size * a.dtype.itemsize for a in (*args, *outs)) if flops else 0

    def body(*refs):
        kernel(*refs[: len(args)], *refs[len(args) + len(after) :])

    return pl.pallas_call(
        body,
        out_shape=list(outs),
        in_specs=[pl.BlockSpec(memory_space=pltpu.VMEM)] * len(args) + [pl.BlockSpec(memory_space=pl.ANY)] * len(after),
        out_specs=[pl.BlockSpec(memory_space=pl.ANY if hbm_out and at == 0 else pltpu.VMEM) for at in range(len(outs))],
        scratch_shapes=list(scratch),
        compiler_params=pltpu.CompilerParams(vmem_limit_bytes=24 * 2**20),
        cost_estimate=pl.CostEstimate(flops=flops, bytes_accessed=size, transcendentals=0),
    )(*args, *after)


def shaped(shape, dtype=F32):
    return jax.ShapeDtypeStruct(shape, dtype)


def split_kernel(own_ref, *out_refs):
    for out_ref, part in zip(out_refs, split3(own_ref[...])):
        out_ref[...] = part


def first_rows_kernel(names_ref, *refs):
    *part_refs, out_ref = refs
    run = part_refs[0].shape[0]
    present = touched_by(names_ref[0:1, :] - lax.axis_index("strata") * run)(run)
    rank = ranks(jnp.broadcast_to(present, (run, LANES)))[:, :TOUCHED]
    sel = (iota(rank.shape, 1).astype(F32) == rank).astype(F32).astype(BF16)
    hi, mid, lo = [dot(sel, ref[...], TN) for ref in part_refs]
    out_ref[...] = (hi + mid) + lo


def run_names(user_ref, t, k, run):
    return user_ref[t : t + 1, :] - (lax.axis_index("strata") ^ k) * run


def pack_entries(n, t, user_ref, item_ref, rating_ref, count_ref, rank, out_ref):
    run = rank.shape[0]
    compact = jnp.zeros((1, user_ref.shape[1]), F32)
    for k in range(n):
        hot = iota((run, user_ref.shape[1]), 0) == run_names(user_ref, t, k, run)
        value = rank[:, t * n + k : t * n + k + 1] + float(k * TOUCHED)
        compact = compact + jnp.sum(jnp.where(hot, value, 0.0), axis=0, keepdims=True)
    active = iota(compact.shape, 1) < count_ref[0:1, t : t + 1]
    out_ref[0:1, :] = jnp.where(active, compact, -1.0)
    out_ref[1:2, :] = item_ref[t : t + 1, :].astype(F32)
    out_ref[2:3, :] = rating_ref[t : t + 1, :]


def pack_first_kernel(n, user_ref, item_ref, rating_ref, count_ref, rank_ref, codes_ref, out_ref):
    run, width = rank_ref.shape
    lane = iota((run, width), 1)
    present = jnp.zeros((run, width), F32)
    for t in range(user_ref.shape[0]):
        for k in range(n):
            named = touched_by(run_names(user_ref, t, k, run))(run)
            present = jnp.where(lane == t * n + k, named, present)
    rank = ranks(present)
    rank_ref[...] = rank
    codes_ref[...] = rank.T[: codes_ref.shape[0]]
    pack_entries(n, 0, user_ref, item_ref, rating_ref, count_ref, rank, out_ref)


def pack_kernel(n, t, user_ref, item_ref, rating_ref, count_ref, rank_ref, out_ref):
    pack_entries(n, t, user_ref, item_ref, rating_ref, count_ref, rank_ref[...], out_ref)


def block_kernel(v_ref, vh_ref, vl_ref):
    vh_ref[...], vl_ref[...] = split2(v_ref[...])


def entry_tables(entry_ref, touched, items):
    low = touched if entry_ref.shape[0] > touched else 0
    per = (entry_ref.shape[0] - low) // FIELDS
    fields = [
        jnp.concatenate([entry_ref[at : at + 1, :] for at in range(low + f * per, low + (f + 1) * per)], axis=1)
        for f in range(FIELDS)
    ]
    users = fields[0].astype(jnp.int32)
    hot = (iota((touched, users.shape[1]), 0) == users).astype(F32)
    values = split3(fields[2])
    left = [hot.astype(BF16)] + [(hot * v.astype(F32)).astype(BF16) for v in values]
    table = dot(jnp.concatenate(left, axis=0), one_hot(fields[1].astype(jnp.int32), items), NT)
    sums = (table[touched : 2 * touched] + table[2 * touched : 3 * touched]) + table[3 * touched :]
    return table[:touched], sums


def prep_kernel(entry_ref, n_ref, r_ref):
    n_ref[...], r_ref[...] = entry_tables(entry_ref, *n_ref.shape)


def twice(ah, al, bh, bl, dims):
    both = dot(jnp.concatenate([ah, al], axis=0), bh, dims)
    rows = ah.shape[0]
    return (both[:rows] + both[rows:]) + dot(ah, bl, dims)


def tile_kernel(piece, whole, first, *refs):
    rows, refs = refs[: len(piece)], refs[len(piece) :]
    if first:
        (codes_ref, low_ref), refs = refs[:2], refs[2:]
    (vh_ref, vl_ref, n_ref, r_ref), refs = refs[:4], refs[4:]
    outs, factors_ref = refs[: len(piece)], refs[len(piece)]
    vh, vl = vh_ref[...], vl_ref[...]
    parts = []
    for at, k in enumerate(piece):
        if first and k == 0:
            hi, lo = rows[at][...], low_ref[...]
        else:
            hi, lo = split2(rows[at][...])
        if k in whole:
            sel = selector(codes_ref[k : k + 1, :])
            hi, lo = dot(sel, hi, NN).astype(BF16), dot(sel, lo, NN).astype(BF16)
        parts.append((hi, lo))
    uh, ul = [jnp.concatenate(x, axis=0) for x in zip(*parts)]
    n_table, r_table = [
        jnp.concatenate([ref[k * TOUCHED : (k + 1) * TOUCHED, :] for k in piece], axis=0) for ref in (n_ref, r_ref)
    ]
    weights = r_table - n_table * twice(uh, ul, vh, vl, NT)
    wh, wl = split2(weights)
    grads = twice(wh, wl, vh, vl, NN)
    for at, k in enumerate(piece):
        outs[at][:TOUCHED, :] = grads[at * TOUCHED : (at + 1) * TOUCHED]
        if first:
            run = codes_ref.shape[1]
            outs[at][TOUCHED:, :] = jnp.zeros((outs[at].shape[0] - TOUCHED, outs[at].shape[1]), F32)
            n = n_ref.shape[0] // TOUCHED
            for t in range(codes_ref.shape[0] // n):
                outs[at][TOUCHED + t : TOUCHED + t + 1, :run] = codes_ref[t * n + k : t * n + k + 1, :]
    if first:
        items = weights.shape[1]
        factors_ref[:, :items] = weights
        factors_ref[:, items:] = uh.astype(F32) + ul.astype(F32)


def item_update(step, weights, rows, v):
    (wh, wl), (uh, ul) = split2(weights), split2(rows)
    grads = dot(wh, uh, TN) + (dot(wl, uh, TN) + dot(wh, ul, TN))
    return v + step * (grads - 0.1 * v)


def items_kernel(step, count, *refs):
    factors = jnp.concatenate([ref[...] for ref in refs[:count]], axis=0)
    v_ref, *out_refs = refs[count:]
    v = v_ref[...]
    items = v.shape[0]
    v = item_update(step, factors[:, :items], factors[:, items:], v)
    if len(out_refs) == 3:
        out_refs[0][...] = v
    out_refs[-2][...], out_refs[-1][...] = split2(v)


def message_weights(touched, message_ref, vh, vl):
    rows = message_ref[:touched, :]
    uh, ul = split2(rows)
    counted, sums = entry_tables(message_ref, touched, vh.shape[0])
    return rows, sums - counted * twice(uh, ul, vh, vl, NT)


def next_kernel(step, touched, message_ref, v_ref, vh_ref, vl_ref):
    v = v_ref[...]
    rows, weights = message_weights(touched, message_ref, *split2(v))
    vh_ref[...], vl_ref[...] = split2(item_update(step, weights, rows, v))


def home_kernel(step, touched, message_ref, v_ref, vh_ref, vl_ref, out_ref, done_ref, held_ref, sems):
    done_ref[...] = jnp.zeros_like(done_ref)
    rows, weights = message_weights(touched, message_ref, vh_ref[...], vl_ref[...])
    chunk = held_ref.shape[0] // HOME_CHUNKS
    copies = []
    for at in range(HOME_CHUNKS):
        part = slice(at * chunk, (at + 1) * chunk)
        held_ref[part, :] = item_update(step, weights[:, part], rows, v_ref[part, :])
        copies.append(pltpu.make_async_copy(held_ref.at[part], out_ref.at[part], sems.at[at]))
        copies[-1].start()
    for copy in copies:
        copy.wait()


def join_kernel(places, *refs):
    *row_refs, entry_ref, out_ref = refs
    width = out_ref.shape[1]
    at = TOUCHED * sum(len(ks) for ks in places)
    for ks, ref in zip(places, row_refs):
        for i, k in enumerate(ks):
            out_ref[k * TOUCHED : (k + 1) * TOUCHED, :] = ref[i * TOUCHED : (i + 1) * TOUCHED, ref.shape[1] - width :]
    for f in range(entry_ref.shape[0]):
        for low in range(0, entry_ref.shape[1], width):
            out_ref[at : at + 1, :] = entry_ref[f : f + 1, low : low + width]
            at += 1


def owner_kernel(order, t, step, *refs):
    n = len(order)
    parts, refs = refs[:n], refs[n:]
    if t == 0:
        ranked = parts
    else:
        ranked, refs = refs[:n], refs[n:]
    own_ref, out_ref, outs = refs[0], refs[1], refs[2:]
    run = own_ref.shape[0]

    def selectors(sub):
        at = slice(TOUCHED + sub, TOUCHED + sub + 1)
        return jnp.concatenate([selector(ref[at, :run]) for ref in ranked], axis=0)

    grads = pick(selectors(t), jnp.concatenate([part[:TOUCHED, :] for part in parts], axis=0), TN)
    own = own_ref[...]
    own = own + step * (grads - 0.1 * own)
    out_ref[...] = own
    if outs:
        rows = pick(selectors(t + 1), own, NN)
        for at in range(n):
            outs[at][...] = rows[at * TOUCHED : (at + 1) * TOUCHED]


def on_device(user_factors, item_factors, ratings, user_offsets, item_offsets, counts):
    n, row_count = lax.axis_size("strata"), lax.axis_size("rows")
    run, rank = user_factors.shape
    items = item_factors.shape[0]
    subs, entries = ratings.shape
    touched = n * TOUCHED
    ranked_rows = TOUCHED + -(-subs // 8) * 8
    steps = [0.04 / (1.0 + 0.5 * t) for t in range(subs)]
    if subs != 2:
        raise ValueError("two sub-epochs")
    sent = (0, *range(n - 1, 0, -1))
    later_pieces = (sent[: n - n // 4], sent[n - n // 4 :])

    def exchange(value, k, shift=0):
        if k == 0 and shift == 0:
            return value
        pairs = [
            (r * n + s, ((r + shift) % row_count) * n + (s ^ k)) for r in range(row_count) for s in range(n)
        ]
        return lax.ppermute(value, ("rows", "strata"), pairs)

    def prepare(values, flops, after=()):
        return call(prep_kernel, [shaped((touched, items))] * 2, values, flops=flops, after=after)

    def join(places, blocks, entry_rows, flops, after):
        out = shaped((touched + FIELDS * entries // rank, rank))
        return call(functools.partial(join_kernel, places), [out], *blocks, entry_rows, flops=flops, after=after)[0]

    def tile(piece, first, *args, after=()):
        *out, factors = call(
            functools.partial(tile_kernel, piece, whole if first else (), first),
            [shaped((ranked_rows if first else TOUCHED, rank))] * len(piece)
            + [shaped((len(piece) * TOUCHED, items + rank) if first else (8, LANES))],
            *[rows[k] for k in piece], *args, flops=FLOPS["tile%d" % (not first)], after=after,
        )
        grads.update(zip(piece, out))
        return factors

    whole = tuple(k for k in WHOLE if k < n)
    pieces = call(split_kernel, [shaped((run, rank), BF16)] * 3, user_factors, flops=FLOPS["split"])
    rows = [pieces[0]] + [None] * (n - 1)
    picked = []
    for k in range(1, n):
        if k in whole:
            rows[k] = exchange(user_factors, k)
        else:
            picked += call(
                first_rows_kernel, [shaped((TOUCHED, rank))], exchange(user_offsets, k), *pieces,
                flops=FLOPS["first"],
            )
            rows[k] = exchange(picked[-1], k)
    listed = (user_offsets, item_offsets, ratings, counts.reshape(1, subs))
    width = -(-subs * n // LANES) * LANES
    ranked, codes, packed = call(
        functools.partial(pack_first_kernel, n),
        [shaped((run, width)), shaped((subs * n, run)), shaped((FIELDS, entries))],
        *listed, flops=FLOPS["pack"], after=picked,
    )
    entries_first = packed
    tables = prepare(packed, FLOPS["prep0"])
    block_parts = call(
        block_kernel, [shaped(item_factors.shape, BF16)] * 2,
        item_factors, flops=FLOPS["block"], after=picked,
    )
    next_block = exchange(item_factors, 0, 1)

    grads, factors = {}, []
    first_pieces = ((0, 1), tuple(range(n - 1, 1, -1)))
    for piece in first_pieces:
        factors.append(tile(piece, True, codes, pieces[1], *block_parts, *tables, after=factors[-1:]))
    parts = [exchange(grads[k], k) for k in range(n)]
    block, *block_parts = call(
        functools.partial(items_kernel, steps[0], len(factors)),
        [shaped(item_factors.shape)] + [shaped(item_factors.shape, BF16)] * 2,
        *factors, item_factors, flops=FLOPS["items"],
    )
    packed = call(
        functools.partial(pack_kernel, n, 1), [shaped((FIELDS, entries))],
        *listed, ranked, flops=FLOPS["pack1"], after=[block],
    )[0]
    tables = prepare(packed, FLOPS["prep1"])
    joined = join(first_pieces, factors, entries_first, FLOPS["stack"], [])
    next_parts = call(
        functools.partial(next_kernel, steps[0], touched), [shaped(item_factors.shape, BF16)] * 2,
        exchange(joined, 0, 1), next_block, flops=FLOPS["next"],
    )
    ranked = [parts[k] for k in sent]
    own, *mine = call(
        functools.partial(owner_kernel, sent, 0, steps[0]),
        [shaped(user_factors.shape)] + [shaped((TOUCHED, rank))] * n,
        *ranked, user_factors, flops=FLOPS["owner"], after=[block, *tables],
    )

    for k, value in zip(sent, mine):
        rows[k] = exchange(value, k)
    grads = {}
    done = []
    for piece in later_pieces:
        done.append(tile(piece, False, *next_parts, *tables, after=done[-1:]))
    parts = [exchange(grads[k], k) for k in range(n)]
    joined = join([(k,) for k in range(n)], rows, packed, FLOPS["join"], [grads[later_pieces[0][0]]])
    block, after_block = call(
        functools.partial(home_kernel, steps[1], touched), [shaped(block.shape), shaped((8, LANES))],
        exchange(joined, 0, -1), block, *block_parts,
        flops=FLOPS["home"], after=[grads[later_pieces[-1][0]]], hbm_out=True,
        scratch=[pltpu.VMEM(block.shape, F32), pltpu.SemaphoreType.DMA((HOME_CHUNKS,))],
    )
    own = call(
        functools.partial(owner_kernel, sent, 1, steps[1]), [shaped(own.shape)],
        *[parts[k] for k in sent], *[dict(zip(sent, ranked))[k] for k in sent], own, flops=FLOPS["fin"],
        after=[after_block],
    )[0]
    return own, block


def solution(mesh):
    return jax.shard_map(
        on_device,
        mesh=mesh,
        in_specs=(
            P(("rows", "strata"), None),
            P(("rows", "strata"), None),
            P(None, ("rows", "strata")),
            P(None, ("rows", "strata")),
            P(None, ("rows", "strata")),
            P(None, ("rows", "strata")),
        ),
        out_specs=(P(("rows", "strata"), None), P(("rows", "strata"), None)),
        check_vma=False,
    )
```

```python
import functools

import jax
import jax.numpy as jnp
from jax import lax
from jax.experimental import pallas as pl
from jax.experimental.pallas import tpu as pltpu
from jax.sharding import PartitionSpec as P

TOUCHED = 32
WHOLE = (0, 1, 2)

HOME_CHUNKS = 4
FLOPS = dict(
    split=8 * 10**7, first=10**11, pack=14 * 10**8, prep0=9 * 10**8, block=2 * 10**8, tile0=10**9, tile1=8 * 10**8,
    items=9 * 10**8, pack1=5 * 10**8, prep1=9 * 10**8, stack=0, next=2 * 10**9, owner=6 * 10**9, join=0,
    home=25 * 10**8, fin=12 * 10**8,
)

F32 = jnp.float32
BF16 = jnp.bfloat16
LANES = 128
FIELDS = 3

NN = (((1,), (0,)), ((), ()))
NT = (((1,), (1,)), ((), ()))
TN = (((0,), (0,)), ((), ()))


def dot(a, b, dims):
    return lax.dot_general(a, b, dims, preferred_element_type=F32)


def split2(x):
    hi = x.astype(BF16)
    return hi, (x - hi.astype(F32)).astype(BF16)


def split3(x):
    hi = x.astype(BF16)
    rest = x - hi.astype(F32)
    mid = rest.astype(BF16)
    return hi, mid, (rest - mid.astype(F32)).astype(BF16)


def pick(selector, x, dims):
    over = dims[0][0][0]
    return dot(jnp.concatenate([selector, selector], axis=over), jnp.concatenate(split2(x), axis=0), dims)


def iota(shape, dim):
    return lax.broadcasted_iota(jnp.int32, shape, dim)


def one_hot(names, rows):
    blocks = []
    for low in range(0, rows, 256):
        size = min(256, rows - low)
        local = jnp.clip(names - low, -1, 256).astype(F32).astype(BF16)
        row = iota((size, LANES), 0).astype(F32).astype(BF16)
        one, zero = jnp.ones((size, LANES), BF16), jnp.zeros((size, LANES), BF16)
        parts = [
            jnp.where(row == local[:, at : at + LANES], one, zero) for at in range(0, names.shape[1], LANES)
        ]
        blocks.append(jnp.concatenate(parts, axis=1))
    return jnp.concatenate(blocks, axis=0)


def touched_by(names):
    def present(run):
        hot = iota((run, names.shape[1]), 0) == names
        return jnp.max(jnp.where(hot, 1.0, 0.0), axis=1, keepdims=True)

    return present


def ranks(present):
    run = present.shape[0]
    before = (iota((run, run), 0) > iota((run, run), 1)).astype(F32).astype(BF16)
    return jnp.where(present > 0.0, dot(before, present.astype(BF16), NN), -1.0)


def selector(rank):
    return (iota((TOUCHED, rank.shape[1]), 0).astype(F32) == rank).astype(F32).astype(BF16)


def call(kernel, outs, *args, flops=0, after=(), hbm_out=False, scratch=()):
    size = sum(a.size * a.dtype.itemsize for a in (*args, *outs)) if flops else 0

    def body(*refs):
        kernel(*refs[: len(args)], *refs[len(args) + len(after) :])

    return pl.pallas_call(
        body,
        out_shape=list(outs),
        in_specs=[pl.BlockSpec(memory_space=pltpu.VMEM)] * len(args) + [pl.BlockSpec(memory_space=pl.ANY)] * len(after),
        out_specs=[pl.BlockSpec(memory_space=pl.ANY if hbm_out and at == 0 else pltpu.VMEM) for at in range(len(outs))],
        scratch_shapes=list(scratch),
        compiler_params=pltpu.CompilerParams(vmem_limit_bytes=24 * 2**20),
        cost_estimate=pl.CostEstimate(flops=flops, bytes_accessed=size, transcendentals=0),
    )(*args, *after)


def shaped(shape, dtype=F32):
    return jax.ShapeDtypeStruct(shape, dtype)


def split_kernel(own_ref, *out_refs):
    for out_ref, part in zip(out_refs, split2(own_ref[...])):
        out_ref[...] = part


def first_rows_kernel(names_ref, *refs):
    *part_refs, out_ref = refs
    run = part_refs[0].shape[0]
    present = touched_by(names_ref[0:1, :] - lax.axis_index("strata") * run)(run)
    rank = ranks(jnp.broadcast_to(present, (run, LANES)))[:, :TOUCHED]
    sel = (iota(rank.shape, 1).astype(F32) == rank).astype(F32).astype(BF16)
    hi, lo = [dot(sel, ref[...], TN) for ref in part_refs]
    out_ref[...] = hi + lo


def run_names(user_ref, t, k, run):
    return user_ref[t : t + 1, :] - (lax.axis_index("strata") ^ k) * run


def pack_entries(n, t, user_ref, item_ref, rating_ref, count_ref, rank, out_ref):
    run = rank.shape[0]
    compact = jnp.zeros((1, user_ref.shape[1]), F32)
    for k in range(n):
        hot = iota((run, user_ref.shape[1]), 0) == run_names(user_ref, t, k, run)
        value = rank[:, t * n + k : t * n + k + 1] + float(k * TOUCHED)
        compact = compact + jnp.sum(jnp.where(hot, value, 0.0), axis=0, keepdims=True)
    active = iota(compact.shape, 1) < count_ref[0:1, t : t + 1]
    out_ref[0:1, :] = jnp.where(active, compact, -1.0)
    out_ref[1:2, :] = item_ref[t : t + 1, :].astype(F32)
    out_ref[2:3, :] = rating_ref[t : t + 1, :]


def pack_first_kernel(n, user_ref, item_ref, rating_ref, count_ref, rank_ref, codes_ref, out_ref):
    run, width = rank_ref.shape
    lane = iota((run, width), 1)
    present = jnp.zeros((run, width), F32)
    for t in range(user_ref.shape[0]):
        for k in range(n):
            named = touched_by(run_names(user_ref, t, k, run))(run)
            present = jnp.where(lane == t * n + k, named, present)
    rank = ranks(present)
    rank_ref[...] = rank
    codes_ref[...] = rank.T[: codes_ref.shape[0]]
    pack_entries(n, 0, user_ref, item_ref, rating_ref, count_ref, rank, out_ref)


def pack_kernel(n, t, user_ref, item_ref, rating_ref, count_ref, rank_ref, out_ref):
    pack_entries(n, t, user_ref, item_ref, rating_ref, count_ref, rank_ref[...], out_ref)


def block_kernel(v_ref, vh_ref, vl_ref):
    vh_ref[...], vl_ref[...] = split2(v_ref[...])


def entry_tables(entry_ref, touched, items):
    low = touched if entry_ref.shape[0] > touched else 0
    per = (entry_ref.shape[0] - low) // FIELDS
    fields = [
        jnp.concatenate([entry_ref[at : at + 1, :] for at in range(low + f * per, low + (f + 1) * per)], axis=1)
        for f in range(FIELDS)
    ]
    hot = one_hot(fields[0].astype(jnp.int32), touched)
    left = [hot] + [hot * value for value in split2(fields[2])]
    table = dot(jnp.concatenate(left, axis=0), one_hot(fields[1].astype(jnp.int32), items), NT)
    return table[:touched], table[touched : 2 * touched] + table[2 * touched :]


def prep_kernel(entry_ref, n_ref, r_ref):
    n_ref[...], r_ref[...] = entry_tables(entry_ref, *n_ref.shape)


def twice(ah, al, bh, bl, dims):
    both = dot(jnp.concatenate([ah, al], axis=0), bh, dims)
    rows = ah.shape[0]
    return (both[:rows] + both[rows:]) + dot(ah, bl, dims)


def tile_kernel(piece, whole, first, *refs):
    rows, refs = refs[: len(piece)], refs[len(piece) :]
    if first:
        (codes_ref, low_ref), refs = refs[:2], refs[2:]
    (vh_ref, vl_ref, n_ref, r_ref), refs = refs[:4], refs[4:]
    outs, factors_ref = refs[: len(piece)], refs[len(piece)]
    vh, vl = vh_ref[...], vl_ref[...]
    parts = []
    for at, k in enumerate(piece):
        if first and k == 0:
            hi, lo = rows[at][...], low_ref[...]
        else:
            hi, lo = split2(rows[at][...])
        if k in whole:
            sel = selector(codes_ref[k : k + 1, :])
            hi, lo = dot(sel, hi, NN).astype(BF16), dot(sel, lo, NN).astype(BF16)
        parts.append((hi, lo))
    uh, ul = [jnp.concatenate(x, axis=0) for x in zip(*parts)]
    n_table, r_table = [
        jnp.concatenate([ref[k * TOUCHED : (k + 1) * TOUCHED, :] for k in piece], axis=0) for ref in (n_ref, r_ref)
    ]
    weights = r_table - n_table * twice(uh, ul, vh, vl, NT)
    wh, wl = split2(weights)
    grads = twice(wh, wl, vh, vl, NN)
    for at, k in enumerate(piece):
        outs[at][:TOUCHED, :] = grads[at * TOUCHED : (at + 1) * TOUCHED]
        if first:
            run = codes_ref.shape[1]
            outs[at][TOUCHED:, :] = jnp.zeros((outs[at].shape[0] - TOUCHED, outs[at].shape[1]), F32)
            n = n_ref.shape[0] // TOUCHED
            for t in range(codes_ref.shape[0] // n):
                outs[at][TOUCHED + t : TOUCHED + t + 1, :run] = codes_ref[t * n + k : t * n + k + 1, :]
    if first:
        items = weights.shape[1]
        factors_ref[:, :items] = weights
        factors_ref[:, items:] = uh.astype(F32) + ul.astype(F32)


def item_update(step, weights, rows, v):
    (wh, wl), (uh, ul) = split2(weights), split2(rows)
    grads = dot(jnp.concatenate([wh, wl, wh], axis=0), jnp.concatenate([uh, uh, ul], axis=0), TN)
    return v + step * (grads - 0.1 * v)


def items_kernel(step, count, *refs):
    factors = jnp.concatenate([ref[...] for ref in refs[:count]], axis=0)
    v_ref, *out_refs = refs[count:]
    v = v_ref[...]
    items = v.shape[0]
    v = item_update(step, factors[:, :items], factors[:, items:], v)
    if len(out_refs) == 3:
        out_refs[0][...] = v
    out_refs[-2][...], out_refs[-1][...] = split2(v)


def message_weights(touched, message_ref, vh, vl):
    rows = message_ref[:touched, :]
    uh, ul = split2(rows)
    counted, sums = entry_tables(message_ref, touched, vh.shape[0])
    return rows, sums - counted * twice(uh, ul, vh, vl, NT)


def next_kernel(step, touched, message_ref, v_ref, vh_ref, vl_ref):
    v = v_ref[...]
    rows, weights = message_weights(touched, message_ref, *split2(v))
    vh_ref[...], vl_ref[...] = split2(item_update(step, weights, rows, v))


def home_kernel(step, touched, message_ref, v_ref, vh_ref, vl_ref, out_ref, done_ref, held_ref, sems):
    done_ref[...] = jnp.zeros_like(done_ref)
    rows, weights = message_weights(touched, message_ref, vh_ref[...], vl_ref[...])
    chunk = held_ref.shape[0] // HOME_CHUNKS
    copies = []
    for at in range(HOME_CHUNKS):
        part = slice(at * chunk, (at + 1) * chunk)
        held_ref[part, :] = item_update(step, weights[:, part], rows, v_ref[part, :])
        copies.append(pltpu.make_async_copy(held_ref.at[part], out_ref.at[part], sems.at[at]))
        copies[-1].start()
    for copy in copies:
        copy.wait()


def join_kernel(places, *refs):
    *row_refs, entry_ref, out_ref = refs
    width = out_ref.shape[1]
    at = TOUCHED * sum(len(ks) for ks in places)
    for ks, ref in zip(places, row_refs):
        for i, k in enumerate(ks):
            out_ref[k * TOUCHED : (k + 1) * TOUCHED, :] = ref[i * TOUCHED : (i + 1) * TOUCHED, ref.shape[1] - width :]
    for f in range(entry_ref.shape[0]):
        for low in range(0, entry_ref.shape[1], width):
            out_ref[at : at + 1, :] = entry_ref[f : f + 1, low : low + width]
            at += 1


def owner_kernel(order, t, step, *refs):
    n = len(order)
    parts, refs = refs[:n], refs[n:]
    if t == 0:
        ranked = parts
    else:
        ranked, refs = refs[:n], refs[n:]
    own_ref, out_ref, outs = refs[0], refs[1], refs[2:]
    run = own_ref.shape[0]

    def selectors(sub):
        at = slice(TOUCHED + sub, TOUCHED + sub + 1)
        return jnp.concatenate([selector(ref[at, :run]) for ref in ranked], axis=0)

    grads = pick(selectors(t), jnp.concatenate([part[:TOUCHED, :] for part in parts], axis=0), TN)
    own = own_ref[...]
    own = own + step * (grads - 0.1 * own)
    out_ref[...] = own
    if outs:
        rows = pick(selectors(t + 1), own, NN)
        for at in range(n):
            outs[at][...] = rows[at * TOUCHED : (at + 1) * TOUCHED]


def on_device(user_factors, item_factors, ratings, user_offsets, item_offsets, counts):
    n, row_count = lax.axis_size("strata"), lax.axis_size("rows")
    run, rank = user_factors.shape
    items = item_factors.shape[0]
    subs, entries = ratings.shape
    touched = n * TOUCHED
    ranked_rows = TOUCHED + -(-subs // 8) * 8
    steps = [0.04 / (1.0 + 0.5 * t) for t in range(subs)]
    if subs != 2:
        raise ValueError("two sub-epochs")
    sent = (0, *range(n - 1, 0, -1))
    later_pieces = (sent[: n - n // 4], sent[n - n // 4 :])

    def exchange(value, k, shift=0):
        if k == 0 and shift == 0:
            return value
        pairs = [
            (r * n + s, ((r + shift) % row_count) * n + (s ^ k)) for r in range(row_count) for s in range(n)
        ]
        return lax.ppermute(value, ("rows", "strata"), pairs)

    def prepare(values, flops, after=()):
        return call(prep_kernel, [shaped((touched, items))] * 2, values, flops=flops, after=after)

    def join(places, blocks, entry_rows, flops, after):
        out = shaped((touched + FIELDS * entries // rank, rank))
        return call(functools.partial(join_kernel, places), [out], *blocks, entry_rows, flops=flops, after=after)[0]

    def tile(piece, first, *args, after=()):
        *out, factors = call(
            functools.partial(tile_kernel, piece, whole if first else (), first),
            [shaped((ranked_rows if first else TOUCHED, rank))] * len(piece)
            + [shaped((len(piece) * TOUCHED, items + rank) if first else (8, LANES))],
            *[rows[k] for k in piece], *args, flops=FLOPS["tile%d" % (not first)], after=after,
        )
        grads.update(zip(piece, out))
        return factors

    whole = tuple(k for k in WHOLE if k < n)
    pieces = call(split_kernel, [shaped((run, rank), BF16)] * 2, user_factors, flops=FLOPS["split"])
    rows = [pieces[0]] + [None] * (n - 1)
    picked = []
    for k in range(1, n):
        if k in whole:
            rows[k] = exchange(user_factors, k)
        else:
            picked += call(
                first_rows_kernel, [shaped((TOUCHED, rank))], exchange(user_offsets, k), *pieces,
                flops=FLOPS["first"],
            )
            rows[k] = exchange(picked[-1], k)
    listed = (user_offsets, item_offsets, ratings, counts.reshape(1, subs))
    width = -(-subs * n // LANES) * LANES
    ranked, codes, packed = call(
        functools.partial(pack_first_kernel, n),
        [shaped((run, width)), shaped((subs * n, run)), shaped((FIELDS, entries))],
        *listed, flops=FLOPS["pack"], after=picked,
    )
    entries_first = packed
    tables = prepare(packed, FLOPS["prep0"])
    block_parts = call(
        block_kernel, [shaped(item_factors.shape, BF16)] * 2,
        item_factors, flops=FLOPS["block"], after=picked,
    )
    next_block = exchange(item_factors, 0, 1)

    grads, factors = {}, []
    first_pieces = ((0, 1), tuple(range(n - 1, 1, -1)))
    for piece in first_pieces:
        factors.append(tile(piece, True, codes, pieces[1], *block_parts, *tables, after=factors[-1:]))
    parts = [exchange(grads[k], k) for k in range(n)]
    block, *block_parts = call(
        functools.partial(items_kernel, steps[0], len(factors)),
        [shaped(item_factors.shape)] + [shaped(item_factors.shape, BF16)] * 2,
        *factors, item_factors, flops=FLOPS["items"],
    )
    packed = call(
        functools.partial(pack_kernel, n, 1), [shaped((FIELDS, entries))],
        *listed, ranked, flops=FLOPS["pack1"], after=[block],
    )[0]
    tables = prepare(packed, FLOPS["prep1"])
    joined = join(first_pieces, factors, entries_first, FLOPS["stack"], [])
    next_parts = call(
        functools.partial(next_kernel, steps[0], touched), [shaped(item_factors.shape, BF16)] * 2,
        exchange(joined, 0, 1), next_block, flops=FLOPS["next"],
    )
    ranked = [parts[k] for k in sent]
    own, *mine = call(
        functools.partial(owner_kernel, sent, 0, steps[0]),
        [shaped(user_factors.shape)] + [shaped((TOUCHED, rank))] * n,
        *ranked, user_factors, flops=FLOPS["owner"], after=[block, *tables],
    )

    for k, value in zip(sent, mine):
        rows[k] = exchange(value, k)
    grads = {}
    done = []
    for piece in later_pieces:
        done.append(tile(piece, False, *next_parts, *tables, after=done[-1:]))
    parts = [exchange(grads[k], k) for k in range(n)]
    joined = join([(k,) for k in range(n)], rows, packed, FLOPS["join"], [grads[later_pieces[0][0]]])
    block, after_block = call(
        functools.partial(home_kernel, steps[1], touched), [shaped(block.shape), shaped((8, LANES))],
        exchange(joined, 0, -1), block, *block_parts,
        flops=FLOPS["home"], after=[grads[later_pieces[-1][0]]], hbm_out=True,
        scratch=[pltpu.VMEM(block.shape, F32), pltpu.SemaphoreType.DMA((HOME_CHUNKS,))],
    )
    own = call(
        functools.partial(owner_kernel, sent, 1, steps[1]), [shaped(own.shape)],
        *[parts[k] for k in sent], *[dict(zip(sent, ranked))[k] for k in sent], own, flops=FLOPS["fin"],
        after=[after_block],
    )[0]
    return own, block


def solution(mesh):
    return jax.shard_map(
        on_device,
        mesh=mesh,
        in_specs=(
            P(("rows", "strata"), None),
            P(("rows", "strata"), None),
            P(None, ("rows", "strata")),
            P(None, ("rows", "strata")),
            P(None, ("rows", "strata")),
            P(None, ("rows", "strata")),
        ),
        out_specs=(P(("rows", "strata"), None), P(("rows", "strata"), None)),
        check_vma=False,
    )
```

```python
import functools

import jax
import jax.numpy as jnp
from jax import lax
from jax.experimental import pallas as pl
from jax.experimental.pallas import tpu as pltpu
from jax.sharding import PartitionSpec as P

TOUCHED = 32
WHOLE = (0, 1, 2)

HOME_CHUNKS = 2
FLOPS = dict(
    split=8 * 10**7, first=10**11, pack=14 * 10**8, prep0=9 * 10**8, block=2 * 10**8, tile0=10**9, tile1=8 * 10**8,
    items=9 * 10**8, pack1=5 * 10**8, prep1=9 * 10**8, stack=0, next=2 * 10**9, owner=6 * 10**9, join=0,
    home=25 * 10**8, fin=12 * 10**8,
)

F32 = jnp.float32
BF16 = jnp.bfloat16
LANES = 128
FIELDS = 3

NN = (((1,), (0,)), ((), ()))
NT = (((1,), (1,)), ((), ()))
TN = (((0,), (0,)), ((), ()))


def dot(a, b, dims):
    return lax.dot_general(a, b, dims, preferred_element_type=F32)


def split2(x):
    hi = x.astype(BF16)
    return hi, (x - hi.astype(F32)).astype(BF16)


def pick(selector, x, dims):
    over = dims[0][0][0]
    return dot(jnp.concatenate([selector, selector], axis=over), jnp.concatenate(split2(x), axis=0), dims)


def iota(shape, dim):
    return lax.broadcasted_iota(jnp.int32, shape, dim)


def one_hot(names, rows):
    return (iota((rows, names.shape[1]), 0) == names).astype(F32).astype(BF16)


def touched_by(names):
    def present(run):
        hot = iota((run, names.shape[1]), 0) == names
        return jnp.max(jnp.where(hot, 1.0, 0.0), axis=1, keepdims=True)

    return present


def ranks(present):
    run = present.shape[0]
    before = (iota((run, run), 0) > iota((run, run), 1)).astype(F32).astype(BF16)
    return jnp.where(present > 0.0, dot(before, present.astype(BF16), NN), -1.0)


def selector(rank):
    return (iota((TOUCHED, rank.shape[1]), 0).astype(F32) == rank).astype(F32).astype(BF16)


def call(kernel, outs, *args, flops=0, after=(), hbm_out=False, scratch=()):
    size = sum(a.size * a.dtype.itemsize for a in (*args, *outs)) if flops else 0

    def body(*refs):
        kernel(*refs[: len(args)], *refs[len(args) + len(after) :])

    return pl.pallas_call(
        body,
        out_shape=list(outs),
        in_specs=[pl.BlockSpec(memory_space=pltpu.VMEM)] * len(args) + [pl.BlockSpec(memory_space=pl.ANY)] * len(after),
        out_specs=[pl.BlockSpec(memory_space=pl.ANY if hbm_out and at == 0 else pltpu.VMEM) for at in range(len(outs))],
        scratch_shapes=list(scratch),
        compiler_params=pltpu.CompilerParams(vmem_limit_bytes=24 * 2**20),
        cost_estimate=pl.CostEstimate(flops=flops, bytes_accessed=size, transcendentals=0),
    )(*args, *after)


def shaped(shape, dtype=F32):
    return jax.ShapeDtypeStruct(shape, dtype)


def split_kernel(own_ref, *out_refs):
    for out_ref, part in zip(out_refs, split2(own_ref[...])):
        out_ref[...] = part


def first_rows_kernel(names_ref, *refs):
    *part_refs, out_ref = refs
    run = part_refs[0].shape[0]
    present = touched_by(names_ref[0:1, :] - lax.axis_index("strata") * run)(run)
    rank = ranks(jnp.broadcast_to(present, (run, LANES)))[:, :TOUCHED]
    sel = (iota(rank.shape, 1).astype(F32) == rank).astype(F32).astype(BF16)
    hi, lo = [dot(sel, ref[...], TN) for ref in part_refs]
    out_ref[...] = hi + lo


def run_names(user_ref, t, k, run):
    return user_ref[t : t + 1, :] - (lax.axis_index("strata") ^ k) * run


def pack_entries(n, t, user_ref, item_ref, rating_ref, count_ref, rank, out_ref):
    run = rank.shape[0]
    compact = jnp.zeros((1, user_ref.shape[1]), F32)
    for k in range(n):
        hot = iota((run, user_ref.shape[1]), 0) == run_names(user_ref, t, k, run)
        value = rank[:, t * n + k : t * n + k + 1] + float(k * TOUCHED)
        compact = compact + jnp.sum(jnp.where(hot, value, 0.0), axis=0, keepdims=True)
    active = iota(compact.shape, 1) < count_ref[0:1, t : t + 1]
    out_ref[0:1, :] = jnp.where(active, compact, -1.0)
    out_ref[1:2, :] = item_ref[t : t + 1, :].astype(F32)
    out_ref[2:3, :] = rating_ref[t : t + 1, :]


def pack_first_kernel(n, user_ref, item_ref, rating_ref, count_ref, rank_ref, codes_ref, out_ref):
    run, width = rank_ref.shape
    lane = iota((run, width), 1)
    present = jnp.zeros((run, width), F32)
    for t in range(user_ref.shape[0]):
        for k in range(n):
            named = touched_by(run_names(user_ref, t, k, run))(run)
            present = jnp.where(lane == t * n + k, named, present)
    rank = ranks(present)
    rank_ref[...] = rank
    codes_ref[...] = rank.T[: codes_ref.shape[0]]
    pack_entries(n, 0, user_ref, item_ref, rating_ref, count_ref, rank, out_ref)


def pack_kernel(n, t, user_ref, item_ref, rating_ref, count_ref, rank_ref, out_ref):
    pack_entries(n, t, user_ref, item_ref, rating_ref, count_ref, rank_ref[...], out_ref)


def block_kernel(v_ref, vh_ref, vl_ref):
    vh_ref[...], vl_ref[...] = split2(v_ref[...])


def entry_tables(entry_ref, touched, items):
    low = touched if entry_ref.shape[0] > touched else 0
    per = (entry_ref.shape[0] - low) // FIELDS
    fields = [
        jnp.concatenate([entry_ref[at : at + 1, :] for at in range(low + f * per, low + (f + 1) * per)], axis=1)
        for f in range(FIELDS)
    ]
    hot = (iota((touched, entry_ref.shape[1] * per), 0) == fields[0].astype(jnp.int32)).astype(F32)
    left = [hot.astype(BF16)] + [(hot * value.astype(F32)).astype(BF16) for value in split2(fields[2])]
    table = dot(jnp.concatenate(left, axis=0), one_hot(fields[1].astype(jnp.int32), items), NT)
    return table[:touched], table[touched : 2 * touched] + table[2 * touched :]


def prep_kernel(entry_ref, n_ref, r_ref):
    n_ref[...], r_ref[...] = entry_tables(entry_ref, *n_ref.shape)


def twice(ah, al, bh, bl, dims):
    both = dot(jnp.concatenate([ah, al], axis=0), bh, dims)
    rows = ah.shape[0]
    return (both[:rows] + both[rows:]) + dot(ah, bl, dims)


def tile_kernel(piece, whole, first, *refs):
    rows, refs = refs[: len(piece)], refs[len(piece) :]
    if first:
        (codes_ref, low_ref), refs = refs[:2], refs[2:]
    (vh_ref, vl_ref, n_ref, r_ref), refs = refs[:4], refs[4:]
    outs, factors_ref = refs[: len(piece)], refs[len(piece)]
    vh, vl = vh_ref[...], vl_ref[...]
    parts = []
    for at, k in enumerate(piece):
        if first and k == 0:
            hi, lo = rows[at][...], low_ref[...]
        else:
            hi, lo = split2(rows[at][...])
        if k in whole:
            sel = selector(codes_ref[k : k + 1, :])
            hi, lo = dot(sel, hi, NN).astype(BF16), dot(sel, lo, NN).astype(BF16)
        parts.append((hi, lo))
    uh, ul = [jnp.concatenate(x, axis=0) for x in zip(*parts)]
    n_table, r_table = [
        jnp.concatenate([ref[k * TOUCHED : (k + 1) * TOUCHED, :] for k in piece], axis=0) for ref in (n_ref, r_ref)
    ]
    weights = r_table - n_table * twice(uh, ul, vh, vl, NT)
    wh, wl = split2(weights)
    grads = twice(wh, wl, vh, vl, NN)
    for at, k in enumerate(piece):
        outs[at][:TOUCHED, :] = grads[at * TOUCHED : (at + 1) * TOUCHED]
        if first:
            run = codes_ref.shape[1]
            outs[at][TOUCHED:, :] = jnp.zeros((outs[at].shape[0] - TOUCHED, outs[at].shape[1]), F32)
            n = n_ref.shape[0] // TOUCHED
            for t in range(codes_ref.shape[0] // n):
                outs[at][TOUCHED + t : TOUCHED + t + 1, :run] = codes_ref[t * n + k : t * n + k + 1, :]
    if first:
        items = weights.shape[1]
        factors_ref[:, :items] = weights
        factors_ref[:, items:] = uh.astype(F32) + ul.astype(F32)


def item_update(step, weights, rows, v):
    (wh, wl), (uh, ul) = split2(weights), split2(rows)
    grads = dot(jnp.concatenate([wh, wl, wh], axis=0), jnp.concatenate([uh, uh, ul], axis=0), TN)
    return v + step * (grads - 0.1 * v)


def items_kernel(step, count, *refs):
    factors = jnp.concatenate([ref[...] for ref in refs[:count]], axis=0)
    v_ref, *out_refs = refs[count:]
    v = v_ref[...]
    items = v.shape[0]
    v = item_update(step, factors[:, :items], factors[:, items:], v)
    if len(out_refs) == 3:
        out_refs[0][...] = v
    out_refs[-2][...], out_refs[-1][...] = split2(v)


def message_weights(touched, message_ref, vh, vl):
    rows = message_ref[:touched, :]
    uh, ul = split2(rows)
    counted, sums = entry_tables(message_ref, touched, vh.shape[0])
    return rows, sums - counted * twice(uh, ul, vh, vl, NT)


def next_kernel(step, touched, message_ref, v_ref, vh_ref, vl_ref):
    v = v_ref[...]
    rows, weights = message_weights(touched, message_ref, *split2(v))
    vh_ref[...], vl_ref[...] = split2(item_update(step, weights, rows, v))


def home_kernel(step, touched, message_ref, v_ref, vh_ref, vl_ref, out_ref, done_ref, held_ref, sems):
    done_ref[...] = jnp.zeros_like(done_ref)
    rows, weights = message_weights(touched, message_ref, vh_ref[...], vl_ref[...])
    chunk = held_ref.shape[0] // HOME_CHUNKS
    copies = []
    for at in range(HOME_CHUNKS):
        part = slice(at * chunk, (at + 1) * chunk)
        held_ref[part, :] = item_update(step, weights[:, part], rows, v_ref[part, :])
        copies.append(pltpu.make_async_copy(held_ref.at[part], out_ref.at[part], sems.at[at]))
        copies[-1].start()
    for copy in copies:
        copy.wait()


def join_kernel(places, *refs):
    *row_refs, entry_ref, out_ref = refs
    width = out_ref.shape[1]
    at = TOUCHED * sum(len(ks) for ks in places)
    for ks, ref in zip(places, row_refs):
        for i, k in enumerate(ks):
            out_ref[k * TOUCHED : (k + 1) * TOUCHED, :] = ref[i * TOUCHED : (i + 1) * TOUCHED, ref.shape[1] - width :]
    for f in range(entry_ref.shape[0]):
        for low in range(0, entry_ref.shape[1], width):
            out_ref[at : at + 1, :] = entry_ref[f : f + 1, low : low + width]
            at += 1


def owner_kernel(order, t, step, *refs):
    n = len(order)
    parts, refs = refs[:n], refs[n:]
    if t == 0:
        ranked = parts
    else:
        ranked, refs = refs[:n], refs[n:]
    own_ref, out_ref, outs = refs[0], refs[1], refs[2:]
    run = own_ref.shape[0]

    def selectors(sub):
        at = slice(TOUCHED + sub, TOUCHED + sub + 1)
        return jnp.concatenate([selector(ref[at, :run]) for ref in ranked], axis=0)

    grads = pick(selectors(t), jnp.concatenate([part[:TOUCHED, :] for part in parts], axis=0), TN)
    own = own_ref[...]
    own = own + step * (grads - 0.1 * own)
    out_ref[...] = own
    if outs:
        rows = pick(selectors(t + 1), own, NN)
        for at in range(n):
            outs[at][...] = rows[at * TOUCHED : (at + 1) * TOUCHED]


def on_device(user_factors, item_factors, ratings, user_offsets, item_offsets, counts):
    n, row_count = lax.axis_size("strata"), lax.axis_size("rows")
    run, rank = user_factors.shape
    items = item_factors.shape[0]
    subs, entries = ratings.shape
    touched = n * TOUCHED
    ranked_rows = TOUCHED + -(-subs // 8) * 8
    steps = [0.04 / (1.0 + 0.5 * t) for t in range(subs)]
    if subs != 2:
        raise ValueError("two sub-epochs")
    sent = (0, *range(n - 1, 0, -1))
    later_pieces = (sent[: n - n // 4], sent[n - n // 4 :])

    def exchange(value, k, shift=0):
        if k == 0 and shift == 0:
            return value
        pairs = [
            (r * n + s, ((r + shift) % row_count) * n + (s ^ k)) for r in range(row_count) for s in range(n)
        ]
        return lax.ppermute(value, ("rows", "strata"), pairs)

    def prepare(values, flops, after=()):
        return call(prep_kernel, [shaped((touched, items))] * 2, values, flops=flops, after=after)

    def join(places, blocks, entry_rows, flops, after):
        out = shaped((touched + FIELDS * entries // rank, rank))
        return call(functools.partial(join_kernel, places), [out], *blocks, entry_rows, flops=flops, after=after)[0]

    def tile(piece, first, *args, after=()):
        *out, factors = call(
            functools.partial(tile_kernel, piece, whole if first else (), first),
            [shaped((ranked_rows if first else TOUCHED, rank))] * len(piece)
            + [shaped((len(piece) * TOUCHED, items + rank) if first else (8, LANES))],
            *[rows[k] for k in piece], *args, flops=FLOPS["tile%d" % (not first)], after=after,
        )
        grads.update(zip(piece, out))
        return factors

    whole = tuple(k for k in WHOLE if k < n)
    pieces = call(split_kernel, [shaped((run, rank), BF16)] * 2, user_factors, flops=FLOPS["split"])
    rows = [pieces[0]] + [None] * (n - 1)
    picked = []
    for k in range(1, n):
        if k in whole:
            rows[k] = exchange(user_factors, k)
        else:
            picked += call(
                first_rows_kernel, [shaped((TOUCHED, rank))], exchange(user_offsets, k), *pieces,
                flops=FLOPS["first"],
            )
            rows[k] = exchange(picked[-1], k)
    listed = (user_offsets, item_offsets, ratings, counts.reshape(1, subs))
    width = -(-subs * n // LANES) * LANES
    ranked, codes, packed = call(
        functools.partial(pack_first_kernel, n),
        [shaped((run, width)), shaped((subs * n, run)), shaped((FIELDS, entries))],
        *listed, flops=FLOPS["pack"], after=picked,
    )
    entries_first = packed
    tables = prepare(packed, FLOPS["prep0"])
    block_parts = call(
        block_kernel, [shaped(item_factors.shape, BF16)] * 2,
        item_factors, flops=FLOPS["block"], after=picked,
    )
    next_block = exchange(item_factors, 0, 1)

    grads, factors = {}, []
    first_pieces = ((0, 1), tuple(range(n - 1, 1, -1)))
    for piece in first_pieces:
        factors.append(tile(piece, True, codes, pieces[1], *block_parts, *tables, after=factors[-1:]))
    parts = [exchange(grads[k], k) for k in range(n)]
    block, *block_parts = call(
        functools.partial(items_kernel, steps[0], len(factors)),
        [shaped(item_factors.shape)] + [shaped(item_factors.shape, BF16)] * 2,
        *factors, item_factors, flops=FLOPS["items"],
    )
    packed = call(
        functools.partial(pack_kernel, n, 1), [shaped((FIELDS, entries))],
        *listed, ranked, flops=FLOPS["pack1"], after=[block],
    )[0]
    tables = prepare(packed, FLOPS["prep1"])
    joined = join(first_pieces, factors, entries_first, FLOPS["stack"], [])
    next_parts = call(
        functools.partial(next_kernel, steps[0], touched), [shaped(item_factors.shape, BF16)] * 2,
        exchange(joined, 0, 1), next_block, flops=FLOPS["next"],
    )
    ranked = [parts[k] for k in sent]
    own, *mine = call(
        functools.partial(owner_kernel, sent, 0, steps[0]),
        [shaped(user_factors.shape)] + [shaped((TOUCHED, rank))] * n,
        *ranked, user_factors, flops=FLOPS["owner"], after=[block, *tables],
    )

    for k, value in zip(sent, mine):
        rows[k] = exchange(value, k)
    grads = {}
    done = []
    for piece in later_pieces:
        done.append(tile(piece, False, *next_parts, *tables, after=done[-1:]))
    parts = [exchange(grads[k], k) for k in range(n)]
    joined = join([(k,) for k in range(n)], rows, packed, FLOPS["join"], [grads[later_pieces[0][0]]])
    block, after_block = call(
        functools.partial(home_kernel, steps[1], touched), [shaped(block.shape), shaped((8, LANES))],
        exchange(joined, 0, -1), block, *block_parts,
        flops=FLOPS["home"], after=[grads[later_pieces[-1][0]]], hbm_out=True,
        scratch=[pltpu.VMEM(block.shape, F32), pltpu.SemaphoreType.DMA((HOME_CHUNKS,))],
    )
    own = call(
        functools.partial(owner_kernel, sent, 1, steps[1]), [shaped(own.shape)],
        *[parts[k] for k in sent], *[dict(zip(sent, ranked))[k] for k in sent], own, flops=FLOPS["fin"],
        after=[after_block],
    )[0]
    return own, block


def solution(mesh):
    return jax.shard_map(
        on_device,
        mesh=mesh,
        in_specs=(
            P(("rows", "strata"), None),
            P(("rows", "strata"), None),
            P(None, ("rows", "strata")),
            P(None, ("rows", "strata")),
            P(None, ("rows", "strata")),
            P(None, ("rows", "strata")),
        ),
        out_specs=(P(("rows", "strata"), None), P(("rows", "strata"), None)),
        check_vma=False,
    )
```

```python
import functools

import jax
import jax.numpy as jnp
from jax import lax
from jax.experimental import pallas as pl
from jax.experimental.pallas import tpu as pltpu
from jax.sharding import PartitionSpec as P

TOUCHED = 32
WHOLE = (0, 1, 2)

HOME_CHUNKS = 2
FLOPS = dict(
    split=8 * 10**7, first=10**11, pack=14 * 10**8, prep0=9 * 10**8, block=2 * 10**8, tile0=10**9, tile1=8 * 10**8,
    items=9 * 10**8, pack1=5 * 10**8, prep1=9 * 10**8, stack=0, next=2 * 10**9, owner=6 * 10**9, join=0,
    home=25 * 10**8, fin=12 * 10**8,
)

F32 = jnp.float32
BF16 = jnp.bfloat16
LANES = 128
FIELDS = 3

NN = (((1,), (0,)), ((), ()))
NT = (((1,), (1,)), ((), ()))
TN = (((0,), (0,)), ((), ()))


def dot(a, b, dims):
    return lax.dot_general(a, b, dims, preferred_element_type=F32)


def split2(x):
    hi = x.astype(BF16)
    return hi, (x - hi.astype(F32)).astype(BF16)


def pick(selector, x, dims):
    over = dims[0][0][0]
    return dot(jnp.concatenate([selector, selector], axis=over), jnp.concatenate(split2(x), axis=0), dims)


def iota(shape, dim):
    return lax.broadcasted_iota(jnp.int32, shape, dim)


def one_hot(names, rows):
    return (iota((rows, names.shape[1]), 0) == names).astype(F32).astype(BF16)


def touched_by(names):
    def present(run):
        hot = iota((run, names.shape[1]), 0) == names
        return jnp.max(jnp.where(hot, 1.0, 0.0), axis=1, keepdims=True)

    return present


def ranks(present):
    run = present.shape[0]
    before = (iota((run, run), 0) > iota((run, run), 1)).astype(F32).astype(BF16)
    return jnp.where(present > 0.0, dot(before, present.astype(BF16), NN), -1.0)


def selector(rank):
    return (iota((TOUCHED, rank.shape[1]), 0).astype(F32) == rank).astype(F32).astype(BF16)


def call(kernel, outs, *args, flops=0, after=(), hbm_out=False, scratch=()):
    size = sum(a.size * a.dtype.itemsize for a in (*args, *outs)) if flops else 0

    def body(*refs):
        kernel(*refs[: len(args)], *refs[len(args) + len(after) :])

    return pl.pallas_call(
        body,
        out_shape=list(outs),
        in_specs=[pl.BlockSpec(memory_space=pltpu.VMEM)] * len(args) + [pl.BlockSpec(memory_space=pl.ANY)] * len(after),
        out_specs=[pl.BlockSpec(memory_space=pl.ANY if hbm_out and at == 0 else pltpu.VMEM) for at in range(len(outs))],
        scratch_shapes=list(scratch),
        compiler_params=pltpu.CompilerParams(vmem_limit_bytes=24 * 2**20),
        cost_estimate=pl.CostEstimate(flops=flops, bytes_accessed=size, transcendentals=0),
    )(*args, *after)


def shaped(shape, dtype=F32):
    return jax.ShapeDtypeStruct(shape, dtype)


def split_kernel(own_ref, *out_refs):
    for out_ref, part in zip(out_refs, split2(own_ref[...])):
        out_ref[...] = part


def first_rows_kernel(names_ref, *refs):
    *part_refs, out_ref = refs
    run = part_refs[0].shape[0]
    present = touched_by(names_ref[0:1, :] - lax.axis_index("strata") * run)(run)
    rank = ranks(jnp.broadcast_to(present, (run, LANES)))[:, :TOUCHED]
    sel = (iota(rank.shape, 1).astype(F32) == rank).astype(F32).astype(BF16)
    hi, lo = [dot(sel, ref[...], TN) for ref in part_refs]
    out_ref[...] = hi + lo


def run_names(user_ref, t, k, run):
    return user_ref[t : t + 1, :] - (lax.axis_index("strata") ^ k) * run


def pack_entries(n, t, user_ref, item_ref, rating_ref, count_ref, rank, out_ref):
    run = rank.shape[0]
    compact = jnp.zeros((1, user_ref.shape[1]), F32)
    for k in range(n):
        hot = iota((run, user_ref.shape[1]), 0) == run_names(user_ref, t, k, run)
        value = rank[:, t * n + k : t * n + k + 1] + float(k * TOUCHED)
        compact = compact + jnp.sum(jnp.where(hot, value, 0.0), axis=0, keepdims=True)
    active = iota(compact.shape, 1) < count_ref[0:1, t : t + 1]
    out_ref[0:1, :] = jnp.where(active, compact, -1.0)
    out_ref[1:2, :] = item_ref[t : t + 1, :].astype(F32)
    out_ref[2:3, :] = rating_ref[t : t + 1, :]


def pack_first_kernel(n, user_ref, item_ref, rating_ref, count_ref, rank_ref, codes_ref, out_ref):
    run, width = rank_ref.shape
    lane = iota((run, width), 1)
    present = jnp.zeros((run, width), F32)
    for t in range(user_ref.shape[0]):
        for k in range(n):
            named = touched_by(run_names(user_ref, t, k, run))(run)
            present = jnp.where(lane == t * n + k, named, present)
    rank = ranks(present)
    rank_ref[...] = rank
    codes_ref[...] = rank.T[: codes_ref.shape[0]]
    pack_entries(n, 0, user_ref, item_ref, rating_ref, count_ref, rank, out_ref)


def pack_kernel(n, t, user_ref, item_ref, rating_ref, count_ref, rank_ref, out_ref):
    pack_entries(n, t, user_ref, item_ref, rating_ref, count_ref, rank_ref[...], out_ref)


def block_kernel(v_ref, vh_ref, vl_ref):
    vh_ref[...], vl_ref[...] = split2(v_ref[...])


def entry_tables(entry_ref, touched, items):
    low = touched if entry_ref.shape[0] > touched else 0
    per = (entry_ref.shape[0] - low) // FIELDS
    fields = [
        jnp.concatenate([entry_ref[at : at + 1, :] for at in range(low + f * per, low + (f + 1) * per)], axis=1)
        for f in range(FIELDS)
    ]
    hot = (iota((touched, entry_ref.shape[1] * per), 0) == fields[0].astype(jnp.int32)).astype(F32)
    left = [hot.astype(BF16)] + [(hot * value.astype(F32)).astype(BF16) for value in split2(fields[2])]
    table = dot(jnp.concatenate(left, axis=0), one_hot(fields[1].astype(jnp.int32), items), NT)
    return table[:touched], table[touched : 2 * touched] + table[2 * touched :]


def prep_kernel(entry_ref, n_ref, r_ref):
    n_ref[...], r_ref[...] = entry_tables(entry_ref, *n_ref.shape)


def twice(ah, al, bh, bl, dims):
    both = dot(jnp.concatenate([ah, al], axis=0), bh, dims)
    rows = ah.shape[0]
    return (both[:rows] + both[rows:]) + dot(ah, bl, dims)


def tile_kernel(piece, whole, first, *refs):
    rows, refs = refs[: len(piece)], refs[len(piece) :]
    if first:
        (codes_ref, low_ref), refs = refs[:2], refs[2:]
    (vh_ref, vl_ref, n_ref, r_ref), refs = refs[:4], refs[4:]
    outs, factors_ref = refs[: len(piece)], refs[len(piece)]
    vh, vl = vh_ref[...], vl_ref[...]
    parts = []
    for at, k in enumerate(piece):
        if first and k == 0:
            hi, lo = rows[at][...], low_ref[...]
        else:
            hi, lo = split2(rows[at][...])
        if k in whole:
            sel = selector(codes_ref[k : k + 1, :])
            hi, lo = dot(sel, hi, NN).astype(BF16), dot(sel, lo, NN).astype(BF16)
        parts.append((hi, lo))
    uh, ul = [jnp.concatenate(x, axis=0) for x in zip(*parts)]
    n_table, r_table = [
        jnp.concatenate([ref[k * TOUCHED : (k + 1) * TOUCHED, :] for k in piece], axis=0) for ref in (n_ref, r_ref)
    ]
    weights = r_table - n_table * twice(uh, ul, vh, vl, NT)
    wh, wl = split2(weights)
    grads = twice(wh, wl, vh, vl, NN)
    for at, k in enumerate(piece):
        outs[at][:TOUCHED, :] = grads[at * TOUCHED : (at + 1) * TOUCHED]
        if first:
            run = codes_ref.shape[1]
            outs[at][TOUCHED:, :] = jnp.zeros((outs[at].shape[0] - TOUCHED, outs[at].shape[1]), F32)
            n = n_ref.shape[0] // TOUCHED
            for t in range(codes_ref.shape[0] // n):
                outs[at][TOUCHED + t : TOUCHED + t + 1, :run] = codes_ref[t * n + k : t * n + k + 1, :]
    if first:
        items = weights.shape[1]
        factors_ref[:, :items] = weights
        factors_ref[:, items:] = uh.astype(F32) + ul.astype(F32)


def item_update(step, weights, rows, v):
    (wh, wl), (uh, ul) = split2(weights), split2(rows)
    grads = dot(jnp.concatenate([wh, wl, wh], axis=0), jnp.concatenate([uh, uh, ul], axis=0), TN)
    return v + step * (grads - 0.1 * v)


def items_kernel(step, count, *refs):
    factors = jnp.concatenate([ref[...] for ref in refs[:count]], axis=0)
    v_ref, *out_refs = refs[count:]
    v = v_ref[...]
    items = v.shape[0]
    v = item_update(step, factors[:, :items], factors[:, items:], v)
    if len(out_refs) == 3:
        out_refs[0][...] = v
    out_refs[-2][...], out_refs[-1][...] = split2(v)


def message_weights(touched, message_ref, vh, vl):
    rows = message_ref[:touched, :]
    uh, ul = split2(rows)
    counted, sums = entry_tables(message_ref, touched, vh.shape[0])
    return rows, sums - counted * twice(uh, ul, vh, vl, NT)


def next_kernel(step, touched, message_ref, v_ref, vh_ref, vl_ref):
    v = v_ref[...]
    rows, weights = message_weights(touched, message_ref, *split2(v))
    vh_ref[...], vl_ref[...] = split2(item_update(step, weights, rows, v))


def home_kernel(step, touched, message_ref, v_ref, vh_ref, vl_ref, out_ref, done_ref, held_ref, sems):
    done_ref[...] = jnp.zeros_like(done_ref)
    rows, weights = message_weights(touched, message_ref, vh_ref[...], vl_ref[...])
    chunk = held_ref.shape[0] // HOME_CHUNKS
    copies = []
    for at in range(HOME_CHUNKS):
        part = slice(at * chunk, (at + 1) * chunk)
        held_ref[part, :] = item_update(step, weights[:, part], rows, v_ref[part, :])
        copies.append(pltpu.make_async_copy(held_ref.at[part], out_ref.at[part], sems.at[at]))
        copies[-1].start()
    for copy in copies:
        copy.wait()


def join_kernel(places, *refs):
    *row_refs, entry_ref, out_ref = refs
    width = out_ref.shape[1]
    at = TOUCHED * sum(len(ks) for ks in places)
    for ks, ref in zip(places, row_refs):
        for i, k in enumerate(ks):
            out_ref[k * TOUCHED : (k + 1) * TOUCHED, :] = ref[i * TOUCHED : (i + 1) * TOUCHED, ref.shape[1] - width :]
    for f in range(entry_ref.shape[0]):
        for low in range(0, entry_ref.shape[1], width):
            out_ref[at : at + 1, :] = entry_ref[f : f + 1, low : low + width]
            at += 1


def owner_kernel(order, t, step, *refs):
    n = len(order)
    parts, refs = refs[:n], refs[n:]
    if t == 0:
        ranked = parts
    else:
        ranked, refs = refs[:n], refs[n:]
    own_ref, out_ref, outs = refs[0], refs[1], refs[2:]
    run = own_ref.shape[0]

    def selectors(sub):
        at = slice(TOUCHED + sub, TOUCHED + sub + 1)
        return jnp.concatenate([selector(ref[at, :run]) for ref in ranked], axis=0)

    grads = pick(selectors(t), jnp.concatenate([part[:TOUCHED, :] for part in parts], axis=0), TN)
    own = own_ref[...]
    own = own + step * (grads - 0.1 * own)
    out_ref[...] = own
    if outs:
        rows = pick(selectors(t + 1), own, NN)
        for at in range(n):
            outs[at][...] = rows[at * TOUCHED : (at + 1) * TOUCHED]


def on_device(user_factors, item_factors, ratings, user_offsets, item_offsets, counts):
    n, row_count = lax.axis_size("strata"), lax.axis_size("rows")
    run, rank = user_factors.shape
    items = item_factors.shape[0]
    subs, entries = ratings.shape
    touched = n * TOUCHED
    ranked_rows = TOUCHED + -(-subs // 8) * 8
    steps = [0.04 / (1.0 + 0.5 * t) for t in range(subs)]
    if subs != 2:
        raise ValueError("two sub-epochs")
    sent = (0, *range(n - 1, 0, -1))
    later_pieces = (sent[: n - n // 4], sent[n - n // 4 :])

    def exchange(value, k, shift=0):
        if k == 0 and shift == 0:
            return value
        pairs = [
            (r * n + s, ((r + shift) % row_count) * n + (s ^ k)) for r in range(row_count) for s in range(n)
        ]
        return lax.ppermute(value, ("rows", "strata"), pairs)

    def prepare(values, flops, after=()):
        return call(prep_kernel, [shaped((touched, items))] * 2, values, flops=flops, after=after)

    def join(places, blocks, entry_rows, flops, after):
        out = shaped((touched + FIELDS * entries // rank, rank))
        return call(functools.partial(join_kernel, places), [out], *blocks, entry_rows, flops=flops, after=after)[0]

    def tile(piece, first, *args, after=()):
        *out, factors = call(
            functools.partial(tile_kernel, piece, whole if first else (), first),
            [shaped((ranked_rows if first else TOUCHED, rank))] * len(piece)
            + [shaped((len(piece) * TOUCHED, items + rank) if first else (8, LANES))],
            *[rows[k] for k in piece], *args, flops=FLOPS["tile%d" % (not first)], after=after,
        )
        grads.update(zip(piece, out))
        return factors

    whole = tuple(k for k in WHOLE if k < n)
    pieces = call(split_kernel, [shaped((run, rank), BF16)] * 2, user_factors, flops=FLOPS["split"])
    rows = [pieces[0]] + [None] * (n - 1)
    picked = []
    for k in range(1, n):
        if k in whole:
            rows[k] = exchange(user_factors, k)
        else:
            picked += call(
                first_rows_kernel, [shaped((TOUCHED, rank))], exchange(user_offsets, k), *pieces,
                flops=FLOPS["first"],
            )
            rows[k] = exchange(picked[-1], k)
    listed = (user_offsets, item_offsets, ratings, counts.reshape(1, subs))
    width = -(-subs * n // LANES) * LANES
    ranked, codes, packed = call(
        functools.partial(pack_first_kernel, n),
        [shaped((run, width)), shaped((subs * n, run)), shaped((FIELDS, entries))],
        *listed, flops=FLOPS["pack"], after=picked,
    )
    entries_first = packed
    tables = prepare(packed, FLOPS["prep0"])
    block_parts = call(
        block_kernel, [shaped(item_factors.shape, BF16)] * 2,
        item_factors, flops=FLOPS["block"], after=picked,
    )
    next_block = exchange(item_factors, 0, 1)

    grads, factors = {}, []
    first_pieces = ((0, 1), tuple(range(n - 1, 1, -1)))
    for piece in first_pieces:
        factors.append(tile(piece, True, codes, pieces[1], *block_parts, *tables, after=factors[-1:]))
    parts = [exchange(grads[k], k) for k in range(n)]
    block, *block_parts = call(
        functools.partial(items_kernel, steps[0], len(factors)),
        [shaped(item_factors.shape)] + [shaped(item_factors.shape, BF16)] * 2,
        *factors, item_factors, flops=FLOPS["items"],
    )
    packed = call(
        functools.partial(pack_kernel, n, 1), [shaped((FIELDS, entries))],
        *listed, ranked, flops=FLOPS["pack1"], after=[block],
    )[0]
    tables = prepare(packed, FLOPS["prep1"])
    joined = join(first_pieces, factors, entries_first, FLOPS["stack"], [block])
    next_parts = call(
        functools.partial(next_kernel, steps[0], touched), [shaped(item_factors.shape, BF16)] * 2,
        exchange(joined, 0, 1), next_block, flops=FLOPS["next"],
    )
    ranked = [parts[k] for k in sent]
    own, *mine = call(
        functools.partial(owner_kernel, sent, 0, steps[0]),
        [shaped(user_factors.shape)] + [shaped((TOUCHED, rank))] * n,
        *ranked, user_factors, flops=FLOPS["owner"], after=[block, *tables],
    )

    for k, value in zip(sent, mine):
        rows[k] = exchange(value, k)
    grads = {}
    done = []
    for piece in later_pieces:
        done.append(tile(piece, False, *next_parts, *tables, after=done[-1:]))
    parts = [exchange(grads[k], k) for k in range(n)]
    joined = join([(k,) for k in range(n)], rows, packed, FLOPS["join"], [grads[later_pieces[0][0]]])
    block, after_block = call(
        functools.partial(home_kernel, steps[1], touched), [shaped(block.shape), shaped((8, LANES))],
        exchange(joined, 0, -1), block, *block_parts,
        flops=FLOPS["home"], after=[grads[later_pieces[-1][0]]], hbm_out=True,
        scratch=[pltpu.VMEM(block.shape, F32), pltpu.SemaphoreType.DMA((HOME_CHUNKS,))],
    )
    own = call(
        functools.partial(owner_kernel, sent, 1, steps[1]), [shaped(own.shape)],
        *[parts[k] for k in sent], *[dict(zip(sent, ranked))[k] for k in sent], own, flops=FLOPS["fin"],
        after=[after_block],
    )[0]
    return own, block


def solution(mesh):
    return jax.shard_map(
        on_device,
        mesh=mesh,
        in_specs=(
            P(("rows", "strata"), None),
            P(("rows", "strata"), None),
            P(None, ("rows", "strata")),
            P(None, ("rows", "strata")),
            P(None, ("rows", "strata")),
            P(None, ("rows", "strata")),
        ),
        out_specs=(P(("rows", "strata"), None), P(("rows", "strata"), None)),
        check_vma=False,
    )
```
